512 devices in a mesh: ctx: 128 (over y, z, core), head: 4 (over x).
Axes of the slice: x: 4, y: 8, z: 8, core: 2. Of those that a mesh axis runs over, the one named last changes fastest.
Arguments:
- queries: bfloat16 [16384, 3072], P(('ctx', 'head')), may hold values from -28 to 28, as said below
- keys: bfloat16 [16384, 3072], P(('ctx', 'head')), may hold values from -14 to 14
- values: bfloat16 [16384, 3072], P(('ctx', 'head')), may hold values from -6 to 6
- band_offsets: int32 [7], replicated, may hold values from -2 to 2
- band_widths: int32 [7], replicated, may hold values from 1 to 4
- block_mask: int32 [7, 8], replicated, may hold values 0 or 1
Outputs:
- attended: bfloat16 [16384, 3072], P(('ctx', 'head'))
The draws below stay inside these ranges and needn't reach their ends.
Inputs may be any that keep to these rules, and one draw needn't show every extreme that they name: `queries`: queries and keys of one head are of order one in most rows.
All inputs are finite; a program needn't handle non-finite values.
Results may differ from the reference program's by a relative error of at most 0.0046.
Values may be sent and summed in bfloat16 or wider, within the bound.
A program may use at most 64 MiB of HBM per device.

```python
import jax
import jax.numpy as jnp
from jax import lax

HEADS = 24
HD = 128
P_SIZE = 128
BLOCKS = 8
NBANDS = 7
D = 3072
FRAMES = 128
TOKENS = 16384


def shared_parts(key):
    base = jax.random.normal(jax.random.fold_in(key, 101), (TOKENS, D), jnp.float32)
    return jnp.clip(base, -4.0, 4.0)


def draw_queries(key, part):
    key = jax.random.fold_in(key, 1)
    own = jnp.clip(jax.random.normal(key, (TOKENS, D), jnp.float32), -4.0, 4.0)
    return own.astype(jnp.bfloat16)


def draw_keys(key, part):
    base = shared_parts(key)
    return base.astype(jnp.bfloat16)


def touch_ends(entries, rng, least, top_value):
    extent = entries.shape
    spot = [jax.random.randint(jax.random.fold_in(rng, axis), (), 0, extent[axis]) for axis in range(len(extent))]
    entries = entries.at[tuple(spot)].set(least)
    longest = extent.index(max(extent))
    spot[longest] = (spot[longest] + 1) % extent[longest]
    return entries.at[tuple(spot)].set(top_value)


def steps_of(rng, shape, cuts, least, top_value):
    def one(dim, parts):
        heights = jax.random.uniform(jax.random.fold_in(jax.random.fold_in(rng, 6), dim), (parts,), jnp.float32, least / len(cuts), top_value / len(cuts))
        return jnp.repeat(jnp.exp(heights), shape[dim] // parts).reshape((-1,) + (1,) * (len(shape) - dim - 1))

    loudness = one(*cuts[0])
    for cut in cuts[1:]:
        loudness = loudness * one(*cut)
    return loudness


def bell_draw(key, shape, scale, bound, cuts=(), kind=jnp.bfloat16):
    values = jax.random.normal(key, shape, jnp.float32) * scale
    if len(cuts) > 0:
        values = steps_of(key, shape, cuts, -0.22, 0.18) * values
    return jnp.clip(values, min=-bound, max=bound).astype(kind)


def setup_inputs(seed: int = 0) -> dict:
    key_of = jax.random.split(jax.random.key(seed), 7)
    queries = draw_queries(jax.random.fold_in(key_of[6], 71), 0)
    keys = draw_keys(jax.random.fold_in(key_of[6], 71), 0)
    values = bell_draw(key_of[2], (TOKENS, D), 1.0, 6.0, ((0, 512),))
    band_offsets = touch_ends(jax.random.randint(key_of[3], (NBANDS,), -2, 3), jax.random.fold_in(key_of[3], 1), -2, 2).astype(jnp.int32)
    band_widths = touch_ends(jax.random.randint(key_of[4], (NBANDS,), 1, 5), jax.random.fold_in(key_of[4], 1), 1, 4).astype(jnp.int32)
    block_mask = touch_ends((jax.random.randint(key_of[5], (NBANDS, BLOCKS), 0, 4) < 3).astype(jnp.int32), jax.random.fold_in(key_of[5], 1), 0, 1)
    return {"queries": queries, "keys": keys, "values": values, "band_offsets": band_offsets, "band_widths": band_widths, "block_mask": block_mask}


NEG = -1.0e30


def block_rule(band_index, band_offsets, band_widths, block_mask):
    block_rows = P_SIZE // BLOCKS
    query_block = jnp.arange(P_SIZE, dtype=jnp.int32) // block_rows
    row_active = block_mask[band_index][query_block]
    distance = query_block[None, :] - query_block[:, None] - band_offsets[band_index]
    allowed = (row_active[:, None] == 1) & (jnp.abs(distance) < band_widths[band_index])
    if band_index == 0:
        allowed = allowed | (query_block[:, None] == query_block[None, :])
    return allowed


def reference(queries, keys, values, band_offsets, band_widths, block_mask):
    query_frames = queries.reshape(FRAMES, P_SIZE, HEADS, HD)
    key_frames = keys.reshape(FRAMES, P_SIZE, HEADS, HD)
    value_frames = values.reshape(FRAMES, P_SIZE, HEADS, HD)
    set_list = [(0, 0)]
    for band_index in range(1, NBANDS):
        reach = 2 ** (band_index - 1)
        set_list.append((-reach, band_index))
        set_list.append((reach, band_index))
    scale = HD ** -0.5

    def one_frame(frame):
        query_now = query_frames[frame].astype(jnp.float32)
        score_list = []
        for offset_frames, band_index in set_list:
            source = frame + offset_frames
            valid = (source >= 0) & (source < FRAMES)
            clipped = jnp.clip(source, 0, FRAMES - 1).astype(jnp.int32)
            key_now = key_frames[clipped].astype(jnp.float32)
            allowed = block_rule(band_index, band_offsets, band_widths, block_mask) & valid
            scores = jnp.einsum('qhd,khd->hqk', query_now, key_now) * scale
            score_list.append((jnp.where(allowed[None], scores, NEG), allowed, clipped))
        peak = score_list[0][0].max(axis=-1)
        for scores, allowed, clipped in score_list[1:]:
            peak = jnp.maximum(peak, scores.max(axis=-1))
        total = jnp.zeros((HEADS, P_SIZE), jnp.float32)
        summed = jnp.zeros((P_SIZE, HEADS, HD), jnp.float32)
        for scores, allowed, clipped in score_list:
            weight = jnp.where(allowed[None], jnp.exp(scores - peak[..., None]), 0.0)
            total = total + weight.sum(axis=-1)
            rounded = weight.astype(jnp.bfloat16).astype(jnp.float32)
            value_now = value_frames[clipped].astype(jnp.float32)
            summed = summed + jnp.einsum('hqk,khd->qhd', rounded, value_now)
        result = summed / jnp.transpose(total)[:, :, None]
        return result.reshape(P_SIZE, D).astype(jnp.bfloat16)

    outputs = lax.map(one_frame, jnp.arange(FRAMES, dtype=jnp.int32))
    return outputs.reshape(TOKENS, D)
```

```python
import functools
import math

import jax
import jax.numpy as jnp
from jax import lax
from jax.experimental import pallas as pl
from jax.experimental.pallas import tpu as pltpu
from jax.sharding import PartitionSpec as P

HD = 128
BLOCKS = 8
NBANDS = 7
HEADS = 3
COLS = HEADS * HD
SCALE = HD ** (-0.5) * math.log2(math.e)
NEG = -1e30
MESH = pl.DeviceIdType.MESH


def place(f):
    f = lax.rem(f + 128, 128)
    return lax.rem(f, 4), lax.div(f, 16), lax.rem(lax.div(f, 4), 2), lax.rem(lax.div(f, 8), 2)


def kernel(
    q_ref, k_ref, v_ref, offset_ref, width_ref, mask_ref, out_ref,
    own, query, xbuf, ybuf, mate, bias, top, total, acc, stage,
    own_sem, query_sem, x_sem, y_sem, mate_sem, out_sem, a2a_send, flow_send, out_send,
):
    ctx, x = lax.axis_index("ctx"), lax.axis_index("head")
    y, z, core = lax.div(ctx, 16), lax.rem(lax.div(ctx, 2), 8), lax.rem(ctx, 2)

    def at(y_, z_, core_):
        return (y_ * 8 + z_) * 2 + core_

    frames = [16 * y + x + 4 * core + 8 * s for s in range(2)]
    home_x, _, home_core, home_slot = place(ctx)
    at_home = (home_x == x) & (home_core == core)
    mate_id = (at(y, z, 1 - core), x)
    up_id = (at(lax.rem(y + 1, 8), z, core), x)
    down_id = (at(lax.rem(y + 7, 8), z, core), x)

    def neighbour(s, step):
        nx, ny, ncore, nslot = place(frames[s] + step)
        return (at(ny, z, ncore), nx), nslot

    after = [neighbour(s, 1) for s in range(2)]
    before = [neighbour(s, -1) for s in range(2)]

    barrier = pltpu.get_barrier_semaphore()

    def greet(device):
        pl.semaphore_signal(barrier, inc=1, device_id=device, device_id_type=MESH)

    def home_of(dz):
        g = lax.rem(z + dz, 8)
        return (at(y, g, home_core), home_x), g

    for device in [mate_id, up_id, down_id] + [n for n, _ in after + before]:
        greet(device)
    for dz in range(1, 8):
        greet(home_of(dz)[0])
    for dt in range(1, 4):
        for s in range(2):
            greet((frames[s], lax.rem(x + dt, 4)))

    @pl.when(jnp.logical_not(at_home))
    def _():
        greet(home_of(0)[0])

    for s in range(2):
        @pl.when(frames[s] != ctx)
        def _():
            greet((frames[s], x))

    pl.semaphore_wait(barrier, 23 - 2 * at_home.astype(jnp.int32))

    token_rows = pl.ds(pl.multiple_of(x * 32, 32), 32)

    def spread(src, dst, recv, send, dz):
        device, _ = home_of(dz)
        if dz:
            pltpu.make_async_remote_copy(
                src_ref=src, dst_ref=dst, send_sem=a2a_send.at[send], recv_sem=recv,
                device_id=device, device_id_type=MESH,
            ).start()
        else:
            @pl.when(at_home)
            def _():
                pltpu.make_async_copy(src, dst, recv).start()

            @pl.when(jnp.logical_not(at_home))
            def _():
                pltpu.make_async_remote_copy(
                    src_ref=src, dst_ref=dst, send_sem=a2a_send.at[3 + send], recv_sem=recv,
                    device_id=device, device_id_type=MESH,
                ).start()

    def spread_head(h):
        for dz in (4, 3, 5, 2, 6, 1, 7, 0):
            g = lax.rem(z + dz, 8)
            columns = pl.ds(pl.multiple_of(g * COLS + h * HD, HD), HD)
            for n, ref in ((0, k_ref), (1, v_ref)):
                spread(ref.at[:, columns], own.at[h, home_slot, n, token_rows], own_sem.at[h], n, dz)

    def spread_queries():
        for dz in (4, 3, 5, 2, 6, 1, 7, 0):
            g = lax.rem(z + dz, 8)
            columns = pl.ds(pl.multiple_of(g * COLS, HD), COLS)
            spread(q_ref.at[:, columns], query.at[home_slot, token_rows], query_sem.at[0], 2, dz)

    def arrived(ref, sem):
        pltpu.make_async_copy(ref, ref, sem).wait()

    def send(src, dst, recv, category, device):
        pltpu.make_async_remote_copy(
            src_ref=src, dst_ref=dst, send_sem=flow_send.at[category], recv_sem=recv,
            device_id=device, device_id_type=MESH,
        ).start()

    def first_sends(h):
        arrived(own.at[h], own_sem.at[h])
        send(own.at[h], ybuf.at[0, h], y_sem.at[0, h], 0, up_id)
        send(own.at[h], ybuf.at[1, h], y_sem.at[1, h], 1, down_id)
        for s in range(2):
            device, slot = after[s]
            send(own.at[h, s], xbuf.at[0, h, slot], x_sem.at[0, h, slot], 2, device)
            device, slot = before[s]
            send(own.at[h, s], xbuf.at[1, h, slot], x_sem.at[1, h, slot], 3, device)
        send(own.at[h], mate.at[h, pl.ds(0, 2)], mate_sem.at[0, h], 4, mate_id)

    def second_sends(h):
        for s in range(2):
            arrived(xbuf.at[0, h, s], x_sem.at[0, h, s])
            device, slot = after[s]
            send(xbuf.at[0, h, s], xbuf.at[2, h, slot], x_sem.at[2, h, slot], 5, device)
            arrived(xbuf.at[1, h, s], x_sem.at[1, h, s])
            device, slot = before[s]
            send(xbuf.at[1, h, s], xbuf.at[3, h, slot], x_sem.at[3, h, slot], 6, device)
        arrived(ybuf.at[0, h], y_sem.at[0, h])
        send(ybuf.at[0, h], ybuf.at[2, h], y_sem.at[2, h], 7, up_id)
        arrived(ybuf.at[1, h], y_sem.at[1, h])
        send(ybuf.at[1, h], ybuf.at[3, h], y_sem.at[3, h], 8, down_id)
        send(ybuf.at[1 - core, h, core], mate.at[h, 2], mate_sem.at[1, h], 9, mate_id)

    for h in range(HEADS):
        spread_head(h)
        if h == 0:
            spread_queries()

    key_block = lax.div(lax.broadcasted_iota(jnp.int32, (HD, HD), 0), 16)
    query_block = lax.div(lax.broadcasted_iota(jnp.int32, (HD, HD), 1), 16)
    distance = key_block - query_block
    for b in range(NBANDS):
        active = jnp.zeros((HD, HD), jnp.int32)
        for block in range(BLOCKS):
            active = jnp.where(query_block == block, mask_ref[b, block], active)
        allowed = (active == 1) & (jnp.abs(distance - offset_ref[b]) < width_ref[b])
        if b == 0:
            allowed = allowed | (distance == 0)
        bias[b] = jnp.where(allowed, 0.0, NEG)
    bias[NBANDS] = jnp.full((HD, HD), NEG, jnp.float32)

    def band(b, s, step):
        source = 16 * y + x + 4 * core + 8 * s + step
        return jnp.where((source >= 0) & (source < 128), b, NBANDS)

    def attend(h, s, sets, first=False):
        q = query[s, :, h * HD : (h + 1) * HD]
        scores = [
            lax.dot_general(ref[0], q, (((1,), (1,)), ((), ())), preferred_element_type=jnp.float32) * SCALE
            + bias[index]
            for ref, index in sets
        ]
        peak = functools.reduce(jnp.maximum, scores).max(axis=0, keepdims=True)
        if not first:
            old = top[h, s]
            peak = jnp.maximum(peak, old)
        weights = [jnp.exp2(score - peak) for score in scores]
        added = functools.reduce(jnp.add, weights).sum(axis=0, keepdims=True)
        summed = [
            lax.dot_general(
                ref[1], weight.astype(jnp.bfloat16), (((0,), (0,)), ((), ())),
                preferred_element_type=jnp.float32,
            )
            for (ref, _), weight in zip(sets, weights)
        ]
        summed = functools.reduce(jnp.add, summed)
        top[h, s] = peak
        if first:
            total[h, s] = added
            acc[h, s] = summed
        else:
            kept = jnp.exp2(old - peak)
            total[h, s] = total[h, s] * kept + added
            acc[h, s] = acc[h, s] * kept + summed

    def both(f):
        for s in range(2):
            f(s)

    def attend_own(h):
        both(lambda s: attend(h, s, [(own.at[h, s], 0), (own.at[h, 1 - s], 4)], first=True))

    def attend_x(h):
        both(lambda s: attend(h, s, [(xbuf.at[0, h, s], band(1, s, -1)), (xbuf.at[1, h, s], band(1, s, 1))]))

    def attend_y(h):
        both(lambda s: attend(h, s, [
            (ybuf.at[0, h, s], band(5, s, -16)),
            (ybuf.at[1, h, s], band(5, s, 16)),
            (ybuf.at[s, h, 1 - s], band(4, s, 8 if s else -8)),
        ]))

    def attend_mate(h):
        arrived(mate.at[h, pl.ds(0, 2)], mate_sem.at[0, h])
        arrived(mate.at[h, 2], mate_sem.at[1, h])
        for s in range(2):
            at_end = core == s
            other = jnp.where(at_end, 2, 1 - s)
            ends = band(3, s, 4 if s else -4)
            attend(h, s, [(mate.at[h, s], 3), (mate.at[h, other], jnp.where(at_end, ends, 3))])

    def attend_x2(h):
        for s in range(2):
            arrived(xbuf.at[2, h, s], x_sem.at[2, h, s])
            arrived(xbuf.at[3, h, s], x_sem.at[3, h, s])
            attend(h, s, [(xbuf.at[2, h, s], band(2, s, -2)), (xbuf.at[3, h, s], band(2, s, 2))])

    def attend_y2(h):
        arrived(ybuf.at[2, h], y_sem.at[2, h])
        arrived(ybuf.at[3, h], y_sem.at[3, h])
        both(lambda s: attend(h, s, [(ybuf.at[2, h, s], band(6, s, -32)), (ybuf.at[3, h, s], band(6, s, 32))]))

    def finish(h):
        columns = pl.ds(pl.multiple_of(z * COLS + h * HD, HD), HD)
        for s in range(2):
            stage[h, s] = (acc[h, s] / total[h, s]).T.astype(jnp.bfloat16)
            for dt in (2, 1, 3, 0):
                t = lax.rem(x + dt, 4)
                src = stage.at[h, s, pl.ds(pl.multiple_of(t * 32, 32), 32)]
                dst = out_ref.at[:, columns]

                def remote(sem):
                    pltpu.make_async_remote_copy(
                        src_ref=src, dst_ref=dst, send_sem=sem, recv_sem=out_sem.at[0],
                        device_id=(frames[s], t), device_id_type=MESH,
                    ).start()

                if dt:
                    remote(out_send.at[2])
                else:
                    @pl.when(frames[s] == ctx)
                    def _():
                        pltpu.make_async_copy(src, dst, out_sem.at[0]).start()

                    @pl.when(frames[s] != ctx)
                    def _():
                        remote(out_send.at[s])

    first_sends(0)
    arrived(query, query_sem.at[0])
    attend_own(0)
    first_sends(1)
    attend_own(1)
    second_sends(0)
    first_sends(2)
    attend_own(2)
    attend_x(0)
    second_sends(1)
    attend_y(0)
    attend_mate(0)
    attend_x(1)
    second_sends(2)
    attend_y(1)
    attend_mate(1)
    attend_x2(0)
    attend_y2(0)
    finish(0)
    attend_x(2)
    attend_y(2)
    attend_mate(2)
    attend_x2(1)
    attend_y2(1)
    finish(1)
    attend_x2(2)
    attend_y2(2)
    finish(2)

    for n, ref in ((0, k_ref), (1, v_ref), (2, q_ref)):
        part = ref.at[:, pl.ds(0, 7 * COLS)]
        arrived(part, a2a_send.at[n])

        @pl.when(jnp.logical_not(at_home))
        def _():
            part = ref.at[:, pl.ds(0, COLS)]
            arrived(part, a2a_send.at[3 + n])

    for category in range(9):
        arrived(own, flow_send.at[category])
    arrived(mate.at[:, 2], flow_send.at[9])
    part = stage.at[:, :, pl.ds(0, 96)]
    arrived(part, out_send.at[2])
    for s in range(2):
        @pl.when(frames[s] != ctx)
        def _():
            part = stage.at[:, s, pl.ds(0, 32)]
            arrived(part, out_send.at[s])
    arrived(out_ref, out_sem.at[0])


def on_device(queries, keys, values, band_offsets, band_widths, block_mask):
    bf16 = jnp.bfloat16
    dma = pltpu.SemaphoreType.DMA
    hbm, smem = pl.BlockSpec(memory_space=pl.ANY), pl.BlockSpec(memory_space=pltpu.SMEM)
    return pl.pallas_call(
        kernel,
        out_shape=jax.ShapeDtypeStruct(queries.shape, bf16),
        in_specs=[hbm] * 3 + [smem] * 3,
        out_specs=hbm,
        scratch_shapes=[
            pltpu.VMEM((HEADS, 2, 2, HD, HD), bf16),
            pltpu.VMEM((2, HD, COLS), bf16),
            pltpu.VMEM((4, HEADS, 2, 2, HD, HD), bf16),
            pltpu.VMEM((4, HEADS, 2, 2, HD, HD), bf16),
            pltpu.VMEM((HEADS, 3, 2, HD, HD), bf16),
            pltpu.VMEM((NBANDS + 1, HD, HD), jnp.float32),
            pltpu.VMEM((HEADS, 2, 1, HD), jnp.float32),
            pltpu.VMEM((HEADS, 2, 1, HD), jnp.float32),
            pltpu.VMEM((HEADS, 2, HD, HD), jnp.float32),
            pltpu.VMEM((HEADS, 2, HD, HD), bf16),
            dma((HEADS,)),
            dma((1,)),
            dma((4, HEADS, 2)),
            dma((4, HEADS)),
            dma((2, HEADS)),
            dma((1,)),
            dma((6,)),
            dma((10,)),
            dma((3,)),
        ],
        compiler_params=pltpu.CompilerParams(
            collective_id=0, has_side_effects=True, vmem_limit_bytes=40 * 2**20
        ),
    )(queries, keys, values, band_offsets, band_widths, block_mask)


def solution(mesh):
    tokens = P(("ctx", "head"), None)
    return jax.shard_map(
        on_device,
        mesh=mesh,
        in_specs=(tokens, tokens, tokens, P(), P(), P()),
        out_specs=tokens,
        check_vma=False,
    )
```

```python
import functools
import itertools
import math

import jax
import jax.numpy as jnp
from jax import lax
from jax.experimental import pallas as pl
from jax.experimental.pallas import tpu as pltpu
from jax.sharding import PartitionSpec as P

HD = 128
BLOCKS = 8
NBANDS = 7
HEADS = 3
COLS = HEADS * HD
SCALE = HD ** (-0.5) * math.log2(math.e)
NEG = -1e30
MESH = pl.DeviceIdType.MESH


def place(f):
    f = lax.rem(f + 128, 128)
    return lax.rem(f, 4), lax.div(f, 16), lax.rem(lax.div(f, 4), 2), lax.rem(lax.div(f, 8), 2)


def kernel(
    q_ref, k_ref, v_ref, offset_hbm, width_hbm, mask_hbm, out_ref,
    offset_ref, width_ref, mask_ref, own, query, xbuf, x2buf, ybuf, mate, bias, top, total, acc, stage,
    table_sem, own_sem, query_sem, x_sem, x2_sem, y_sem, mate_sem, out_sem, a2a_send, flow_send, out_send,
):
    tables = [
        pltpu.make_async_copy(src, dst, table_sem.at[n])
        for n, (src, dst) in enumerate(
            [(offset_hbm, offset_ref), (width_hbm, width_ref), (mask_hbm, mask_ref)]
        )
    ]
    for copy in tables:
        copy.start()
    ctx, x = lax.axis_index("ctx"), lax.axis_index("head")
    y, z, core = lax.div(ctx, 16), lax.rem(lax.div(ctx, 2), 8), lax.rem(ctx, 2)

    def at(y_, z_, core_):
        return (y_ * 8 + z_) * 2 + core_

    frames = [16 * y + x + 4 * core + 8 * s for s in range(2)]
    home_x, _, home_core, home_slot = place(ctx)
    at_home = (home_x == x) & (home_core == core)
    mate_id = (at(y, z, 1 - core), x)
    up_id = (at(lax.rem(y + 1, 8), z, core), x)
    down_id = (at(lax.rem(y + 7, 8), z, core), x)

    def neighbours(step):
        ids, slots = [], []
        for s in range(2):
            nx, ny, ncore, nslot = place(frames[s] + step)
            ids.append((at(ny, z, ncore), nx))
            slots.append(nslot)
        return ids, slots, ncore

    after, after_slot, after_core = neighbours(1)
    before, before_slot, before_core = neighbours(-1)

    barrier = pltpu.get_barrier_semaphore()

    def greet(device):
        pl.semaphore_signal(barrier, inc=1, device_id=device, device_id_type=MESH)

    def home_of(dz):
        return (at(y, lax.rem(z + dz, 8), home_core), home_x)

    for device in [mate_id, up_id, down_id] + after + before:
        greet(device)
    for dz in range(1, 8):
        greet(home_of(dz))
    for dt in range(1, 4):
        for s in range(2):
            greet((frames[s], lax.rem(x + dt, 4)))

    @pl.when(jnp.logical_not(at_home))
    def _():
        greet(home_of(0))

    for s in range(2):
        @pl.when(frames[s] != ctx)
        def _():
            greet((frames[s], x))

    relays = x == 1 + core
    takes = x == 3 * core

    @pl.when(takes)
    def _():
        greet((at(y, z, 1 - core), 2 - core))

    pl.semaphore_wait(barrier, 23 - 2 * at_home.astype(jnp.int32) + relays.astype(jnp.int32))

    token_rows = pl.ds(pl.multiple_of(x * 32, 32), 32)

    def spread(h, n):
        ref = (k_ref, v_ref, q_ref)[n]
        if n == 2:
            dst, recv = query.at[h, home_slot, token_rows], query_sem.at[h]
        else:
            dst, recv = own.at[h, n, home_slot, token_rows], own_sem.at[h, n]

        def remote(src, dz, sem):
            pltpu.make_async_remote_copy(
                src_ref=src, dst_ref=dst, send_sem=a2a_send.at[sem], recv_sem=recv,
                device_id=home_of(dz), device_id_type=MESH,
            ).start()

        for dz in (4, 3, 5, 2, 6, 1, 7, 0):
            g = lax.rem(z + dz, 8)
            src = ref.at[:, pl.ds(pl.multiple_of(g * COLS + h * HD, HD), HD)]
            if dz:
                remote(src, dz, n)
            else:
                @pl.when(at_home)
                def _():
                    pltpu.make_async_copy(src, dst, recv).start()

                @pl.when(jnp.logical_not(at_home))
                def _():
                    remote(src, dz, 3 + n)

    def arrived(ref, sem):
        pltpu.make_async_copy(ref, ref, sem).wait()

    def send(src, dst, recv, category, device):
        pltpu.make_async_remote_copy(
            src_ref=src, dst_ref=dst, send_sem=flow_send.at[category], recv_sem=recv,
            device_id=device, device_id_type=MESH,
        ).start()

    def pick(first, pair):
        return tuple(jnp.where(first, p, q) for p, q in zip(*pair))

    to_first = jnp.where(after_slot[0] == 0, 0, 1)
    to_last = jnp.where(before_slot[1] == 1, 1, 0)
    first_id = pick(to_first == 0, after)
    middle_after_id = pick(to_first == 1, after)
    last_id = pick(to_last == 0, before)
    middle_before_id = pick(to_last == 1, before)

    sends_first = jnp.logical_not((x == 3) & (core == 1))
    sends_last = jnp.logical_not((x == 0) & (core == 0))

    def sends_1(h, n):
        arrived(own.at[h, n], own_sem.at[h, n])
        send(own.at[h, n], ybuf.at[0, h, n], y_sem.at[0, h, n], 0, up_id)
        send(own.at[h, n], ybuf.at[1, h, n], y_sem.at[1, h, n], 1, down_id)
        for s in range(2):
            to = after_slot[s]
            send(own.at[h, n, s], xbuf.at[0, h, n, to], x_sem.at[0, h, n, to], 2, after[s])
            to = before_slot[s]
            send(own.at[h, n, s], xbuf.at[1, h, n, to], x_sem.at[1, h, n, to], 3, before[s])
        send(own.at[h, n], mate.at[h, n, pl.ds(0, 2)], mate_sem.at[0, h, n], 4, mate_id)

    def sends_2(h, n):
        arrived(ybuf.at[0, h, n], y_sem.at[0, h, n])
        send(ybuf.at[0, h, n], ybuf.at[2, h, n], y_sem.at[2, h, n], 9, up_id)
        arrived(ybuf.at[1, h, n], y_sem.at[1, h, n])
        send(ybuf.at[1, h, n], ybuf.at[3, h, n], y_sem.at[3, h, n], 10, down_id)
        end = ybuf.at[1 - core, h, n, core]
        send(end, mate.at[h, n, 2], mate_sem.at[1, h, n], 11, mate_id)

        @pl.when(relays)
        def _():
            send(end, x2buf.at[h, n, 1 - core], x2_sem.at[1 - core, h, n], 14, (at(y, z, 1 - core), 3 - 3 * core))

        for d in range(2):
            for s in range(2):
                arrived(xbuf.at[d, h, n, s], x_sem.at[d, h, n, s])

        @pl.when(sends_first)
        def _():
            send(xbuf.at[0, h, n, to_first], x2buf.at[h, n, 0], x2_sem.at[0, h, n], 5, first_id)

        @pl.when(sends_last)
        def _():
            send(xbuf.at[1, h, n, to_last], x2buf.at[h, n, 1], x2_sem.at[1, h, n], 6, last_id)

        if n == 0:
            @pl.when(after_core == 0)
            def _():
                send(xbuf.at[0, h, n, 1 - to_first], x2buf.at[h, n, 2], x2_sem.at[2, h, n], 7, middle_after_id)
        else:
            @pl.when(before_core == 1)
            def _():
                send(xbuf.at[1, h, n, 1 - to_last], x2buf.at[h, n, 2], x2_sem.at[2, h, n], 8, middle_before_id)

    def sends_3(h, n):
        arrived(x2buf.at[h, n, 0], x2_sem.at[0, h, n])
        arrived(x2buf.at[h, n, 1], x2_sem.at[1, h, n])
        send(x2buf.at[h, n, 1 - core], x2buf.at[h, n, 3], x2_sem.at[3, h, n], 12, mate_id)
        arrived_middle = functools.partial(arrived, x2buf.at[h, n, 2], x2_sem.at[2, h, n])

        @pl.when(core == n)
        def _():
            arrived_middle()
            send(x2buf.at[h, n, 2], x2buf.at[h, n, 2], x2_sem.at[2, h, n], 13, mate_id)

    def fill_bias():
        for copy in tables:
            copy.wait()
        key_block = lax.div(lax.broadcasted_iota(jnp.int32, (HD, HD), 0), 16)
        query_block = lax.div(lax.broadcasted_iota(jnp.int32, (HD, HD), 1), 16)
        distance = key_block - query_block
        for b in range(NBANDS):
            active = jnp.zeros((HD, HD), jnp.int32)
            for block in range(BLOCKS):
                active = jnp.where(query_block == block, mask_ref[b, block], active)
            allowed = (active == 1) & (jnp.abs(distance - offset_ref[b]) < width_ref[b])
            if b == 0:
                allowed = allowed | (distance == 0)
            bias[b] = jnp.where(allowed, 0.0, NEG)
        bias[NBANDS] = jnp.full((HD, HD), NEG, jnp.float32)

    def band(b, s, step):
        source = 16 * y + x + 4 * core + 8 * s + step
        return jnp.where((source >= 0) & (source < 128), b, NBANDS)

    def attend(work, first=False):
        scores = []
        for h, s, sets in work:
            keys = jnp.concatenate([keys[...] for keys, _, _ in sets], axis=0)
            score = lax.dot_general(
                keys, query[h, s], (((1,), (1,)), ((), ())), preferred_element_type=jnp.float32
            )
            scores.append([
                score[n * HD : (n + 1) * HD] * SCALE + bias[index] for n, (_, _, index) in enumerate(sets)
            ])
        values = [[values[...] for _, values, _ in sets] for _, _, sets in work]
        peaks = [functools.reduce(jnp.maximum, score).max(axis=0, keepdims=True) for score in scores]
        if not first:
            old = [(top[h, s], total[h, s], acc[h, s]) for h, s, _ in work]
            peaks = [jnp.maximum(peak, before[0]) for peak, before in zip(peaks, old)]
        results = []
        for n, (score, peak) in enumerate(zip(scores, peaks)):
            weights = [jnp.exp2(part - peak) for part in score]
            added = functools.reduce(jnp.add, weights).sum(axis=0, keepdims=True)
            summed = [
                lax.dot_general(
                    value, weight.astype(jnp.bfloat16), (((0,), (0,)), ((), ())),
                    preferred_element_type=jnp.float32,
                )
                for value, weight in zip(values[n], weights)
            ]
            summed = functools.reduce(jnp.add, summed)
            if not first:
                kept = jnp.exp2(old[n][0] - peak)
                added, summed = old[n][1] * kept + added, old[n][2] * kept + summed
            results.append((peak, added, summed))
        for (h, s, _), (peak, added, summed) in zip(work, results):
            top[h, s], total[h, s], acc[h, s] = peak, added, summed

    def entry(ref, where, index):
        return ref.at[where(0)], ref.at[where(1)], index

    def sets_own(h, s):
        return [entry(own, lambda n: (h, n, s), 0), entry(own, lambda n: (h, n, 1 - s), 4)]

    def sets_x(h, s):
        return [
            entry(xbuf, lambda n: (0, h, n, s), band(1, s, -1)),
            entry(xbuf, lambda n: (1, h, n, s), band(1, s, 1)),
        ]

    def sets_y(h, s):
        return [
            entry(ybuf, lambda n: (0, h, n, s), band(5, s, -16)),
            entry(ybuf, lambda n: (1, h, n, s), band(5, s, 16)),
            entry(ybuf, lambda n: (s, h, n, 1 - s), band(4, s, 8 if s else -8)),
        ]

    def sets_mate(h, s):
        at_end = core == s
        other = jnp.where(at_end, 2, 1 - s)
        ends = band(3, s, 4 if s else -4)
        return [
            entry(mate, lambda n: (h, n, s), 3),
            entry(mate, lambda n: (h, n, other), jnp.where(at_end, ends, 3)),
        ]

    def sets_x2(h, s):
        earlier, later = (0, 3 - core) if s == 0 else (2 + core, 1)
        return [
            entry(x2buf, lambda n: (h, n, earlier), band(2, s, -2)),
            entry(x2buf, lambda n: (h, n, later), band(2, s, 2)),
        ]

    def sets_y2(h, s):
        return [
            entry(ybuf, lambda n: (2, h, n, s), band(6, s, -32)),
            entry(ybuf, lambda n: (3, h, n, s), band(6, s, 32)),
        ]

    def both(h, *kinds, first=False):
        attend([(h, s, sum((sets(h, s) for sets in kinds), [])) for s in range(2)], first)

    def wait_query(h):
        arrived(query.at[h], query_sem.at[h])

    def wait_mate(h):
        for n in range(2):
            arrived(mate.at[h, n, pl.ds(0, 2)], mate_sem.at[0, h, n])
            arrived(mate.at[h, n, 2], mate_sem.at[1, h, n])

    def wait_x2(h):
        for n in range(2):
            @pl.when(core != n)
            def _():
                arrived(x2buf.at[h, n, 2], x2_sem.at[2, h, n])

            arrived(x2buf.at[h, n, 3], x2_sem.at[3, h, n])

    def wait_y2(h):
        for n in range(2):
            arrived(ybuf.at[2, h, n], y_sem.at[2, h, n])
            arrived(ybuf.at[3, h, n], y_sem.at[3, h, n])

    def finish(h):
        columns = pl.ds(pl.multiple_of(z * COLS + h * HD, HD), HD)
        for s in range(2):
            stage[h, s] = (acc[h, s] / total[h, s]).T.astype(jnp.bfloat16)
        for dt, s in itertools.product((2, 1, 3, 0), range(2)):
            t = lax.rem(x + dt, 4)
            src = stage.at[h, s, pl.ds(pl.multiple_of(t * 32, 32), 32)]
            dst = out_ref.at[:, columns]

            def remote(sem):
                pltpu.make_async_remote_copy(
                    src_ref=src, dst_ref=dst, send_sem=sem, recv_sem=out_sem.at[0],
                    device_id=(frames[s], t), device_id_type=MESH,
                ).start()

            if dt:
                remote(out_send.at[2])
            else:
                @pl.when(frames[s] == ctx)
                def _():
                    pltpu.make_async_copy(src, dst, out_sem.at[0]).start()

                @pl.when(frames[s] != ctx)
                def _():
                    remote(out_send.at[s])

    K, V, Q = 0, 1, 2
    for h, n in ((0, K), (0, V), (1, K), (1, V), (0, Q), (2, K), (2, V), (1, Q), (2, Q)):
        spread(h, n)
    fill_bias()
    sends_1(0, K)
    sends_1(0, V)
    sends_1(1, K)
    sends_2(0, K)
    sends_1(1, V)
    sends_2(0, V)
    sends_1(2, K)
    sends_2(1, K)
    sends_1(2, V)
    sends_2(1, V)
    sends_3(0, K)
    sends_3(0, V)
    wait_query(0)
    both(0, sets_own, sets_x, sets_y, first=True)
    sends_2(2, K)
    sends_3(1, K)
    wait_mate(0)
    wait_x2(0)
    both(0, sets_mate, sets_x2)
    wait_query(1)
    both(1, sets_own, sets_x, sets_y, first=True)
    sends_2(2, V)
    sends_3(1, V)
    wait_y2(0)
    both(0, sets_y2)
    finish(0)
    wait_query(2)
    both(2, sets_own, sets_x, sets_y, first=True)
    wait_mate(1)
    wait_x2(1)
    wait_y2(1)
    both(1, sets_mate, sets_x2, sets_y2)
    finish(1)
    sends_3(2, K)
    sends_3(2, V)
    wait_mate(2)
    wait_x2(2)
    both(2, sets_mate, sets_x2)
    wait_y2(2)
    both(2, sets_y2)
    finish(2)

    for n, ref in ((0, k_ref), (1, v_ref), (2, q_ref)):
        part = ref.at[:, pl.ds(0, 7 * COLS)]
        arrived(part, a2a_send.at[n])

        @pl.when(jnp.logical_not(at_home))
        def _():
            part = ref.at[:, pl.ds(0, COLS)]
            arrived(part, a2a_send.at[3 + n])

    half, sixth = own.at[:, :, 0], own.at[:, 0, 0]
    for category in (0, 1, 2, 3, 4, 9, 10):
        arrived(own, flow_send.at[category])
    for category in (11, 12):
        arrived(half, flow_send.at[category])
    for category, sent in ((5, sends_first), (6, sends_last), (14, relays)):
        @pl.when(sent)
        def _():
            arrived(half, flow_send.at[category])

    arrived(sixth, flow_send.at[13])

    @pl.when(after_core == 0)
    def _():
        arrived(sixth, flow_send.at[7])

    @pl.when(before_core == 1)
    def _():
        arrived(sixth, flow_send.at[8])

    part = stage.at[:, :, pl.ds(0, 96)]
    arrived(part, out_send.at[2])
    for s in range(2):
        @pl.when(frames[s] != ctx)
        def _():
            part = stage.at[:, s, pl.ds(0, 32)]
            arrived(part, out_send.at[s])
    arrived(out_ref, out_sem.at[0])


def on_device(queries, keys, values, band_offsets, band_widths, block_mask):
    bf16 = jnp.bfloat16
    dma = pltpu.SemaphoreType.DMA
    hbm = pl.BlockSpec(memory_space=pl.ANY)
    return pl.pallas_call(
        kernel,
        out_shape=jax.ShapeDtypeStruct(queries.shape, bf16),
        in_specs=[hbm] * 6,
        out_specs=hbm,
        scratch_shapes=[
            pltpu.SMEM(band_offsets.shape, jnp.int32),
            pltpu.SMEM(band_widths.shape, jnp.int32),
            pltpu.SMEM(block_mask.shape, jnp.int32),
            pltpu.VMEM((HEADS, 2, 2, HD, HD), bf16),
            pltpu.VMEM((HEADS, 2, HD, HD), bf16),
            pltpu.VMEM((2, HEADS, 2, 2, HD, HD), bf16),
            pltpu.VMEM((HEADS, 2, 4, HD, HD), bf16),
            pltpu.VMEM((4, HEADS, 2, 2, HD, HD), bf16),
            pltpu.VMEM((HEADS, 2, 3, HD, HD), bf16),
            pltpu.VMEM((NBANDS + 1, HD, HD), jnp.float32),
            pltpu.VMEM((HEADS, 2, 1, HD), jnp.float32),
            pltpu.VMEM((HEADS, 2, 1, HD), jnp.float32),
            pltpu.VMEM((HEADS, 2, HD, HD), jnp.float32),
            pltpu.VMEM((HEADS, 2, HD, HD), bf16),
            dma((3,)),
            dma((HEADS, 2)),
            dma((HEADS,)),
            dma((2, HEADS, 2, 2)),
            dma((4, HEADS, 2)),
            dma((4, HEADS, 2)),
            dma((2, HEADS, 2)),
            dma((1,)),
            dma((6,)),
            dma((15,)),
            dma((3,)),
        ],
        compiler_params=pltpu.CompilerParams(
            collective_id=0, has_side_effects=True, vmem_limit_bytes=60 * 2**20
        ),
    )(queries, keys, values, band_offsets, band_widths, block_mask)


def solution(mesh):
    tokens = P(("ctx", "head"), None)
    return jax.shard_map(
        on_device,
        mesh=mesh,
        in_specs=(tokens, tokens, tokens, P(), P(), P()),
        out_specs=tokens,
        check_vma=False,
    )
```

```python
import functools
import itertools
import math

import jax
import jax.numpy as jnp
from jax import lax
from jax.experimental import pallas as pl
from jax.experimental.pallas import tpu as pltpu
from jax.sharding import PartitionSpec as P

HD = 128
BLOCKS = 8
NBANDS = 7
HEADS = 3
COLS = HEADS * HD
SCALE = HD ** (-0.5) * math.log2(math.e)
NEG = -1e30
MESH = pl.DeviceIdType.MESH


def place(f):
    f = lax.rem(f + 128, 128)
    return lax.rem(f, 4), lax.div(f, 16), lax.rem(lax.div(f, 4), 2), lax.rem(lax.div(f, 8), 2)


def kernel(
    q_ref, k_ref, v_ref, offset_hbm, width_hbm, mask_hbm, out_ref,
    offset_ref, width_ref, mask_ref, own, query, xbuf, x2buf, ybuf, y2buf, mate, bias, top, total, acc, stage,
    table_sem, own_sem, query_sem, x_sem, x2_sem, middle_sem, pair_sem, y_sem, y2_sem, mate_sem, out_sem,
    a2a_send, flow_send, out_send,
):
    ctx, x = lax.axis_index("ctx"), lax.axis_index("head")
    y, z, core = lax.div(ctx, 16), lax.rem(lax.div(ctx, 2), 8), lax.rem(ctx, 2)

    def at(y_, z_, core_):
        return (y_ * 8 + z_) * 2 + core_

    frames = [16 * y + x + 4 * core + 8 * s for s in range(2)]
    home_x, _, home_core, home_slot = place(ctx)
    at_home = (home_x == x) & (home_core == core)
    mate_id = (at(y, z, 1 - core), x)
    up_id = (at(lax.rem(y + 1, 8), z, core), x)
    down_id = (at(lax.rem(y + 7, 8), z, core), x)

    def neighbours(step):
        ids, slots = [], []
        for s in range(2):
            nx, ny, ncore, nslot = place(frames[s] + step)
            ids.append((at(ny, z, ncore), nx))
            slots.append(nslot)
        return ids, slots, ncore

    after, after_slot, after_core = neighbours(1)
    before, before_slot, before_core = neighbours(-1)

    barrier = pltpu.get_barrier_semaphore()

    def greet(device):
        pl.semaphore_signal(barrier, inc=1, device_id=device, device_id_type=MESH)

    def home_of(dz):
        return (at(y, lax.rem(z + dz, 8), home_core), home_x)

    for dz in (4, 3, 5, 2, 6, 1, 7):
        greet(home_of(dz))
    for dt in range(1, 4):
        for s in range(2):
            greet((frames[s], lax.rem(x + dt, 4)))

    @pl.when(jnp.logical_not(at_home))
    def _():
        greet(home_of(0))

    for s in range(2):
        @pl.when(frames[s] != ctx)
        def _():
            greet((frames[s], x))

    relays = x == 1 + core
    takes = x == 3 * core

    for device in [mate_id, up_id, down_id] + after + before:
        greet(device)

    @pl.when(takes)
    def _():
        greet((at(y, z, 1 - core), 2 - core))

    tables = [
        pltpu.make_async_copy(src, dst, table_sem.at[n])
        for n, (src, dst) in enumerate(
            [(offset_hbm, offset_ref), (width_hbm, width_ref), (mask_hbm, mask_ref)]
        )
    ]
    for copy in tables:
        copy.start()
    pl.semaphore_wait(barrier, 23 - 2 * at_home.astype(jnp.int32) + relays.astype(jnp.int32))

    token_rows = pl.ds(pl.multiple_of(x * 32, 32), 32)

    def spread(h, n):
        ref = (k_ref, v_ref, q_ref)[n]
        if n == 2:
            dst, recv = query.at[h, home_slot, token_rows], query_sem.at[h]
        else:
            dst, recv = own.at[h, n, home_slot, token_rows], own_sem.at[h, n]

        def remote(src, dz, sem):
            pltpu.make_async_remote_copy(
                src_ref=src, dst_ref=dst, send_sem=a2a_send.at[sem], recv_sem=recv,
                device_id=home_of(dz), device_id_type=MESH,
            ).start()

        for dz in (4, 3, 5, 2, 6, 1, 7, 0):
            g = lax.rem(z + dz, 8)
            src = ref.at[:, pl.ds(pl.multiple_of(g * COLS + h * HD, HD), HD)]
            if dz:
                remote(src, dz, n)
            else:
                @pl.when(at_home)
                def _():
                    pltpu.make_async_copy(src, dst, recv).start()

                @pl.when(jnp.logical_not(at_home))
                def _():
                    remote(src, dz, 3)

    def arrived(ref, sem):
        pltpu.make_async_copy(ref, ref, sem).wait()

    def send(src, dst, recv, category, device):
        pltpu.make_async_remote_copy(
            src_ref=src, dst_ref=dst, send_sem=flow_send.at[category], recv_sem=recv,
            device_id=device, device_id_type=MESH,
        ).start()

    def pick(first, pair):
        return tuple(jnp.where(first, p, q) for p, q in zip(*pair))

    to_first = jnp.where(after_slot[0] == 0, 0, 1)
    to_last = jnp.where(before_slot[1] == 1, 1, 0)
    first_id = pick(to_first == 0, after)
    middle_after_id = pick(to_first == 1, after)
    last_id = pick(to_last == 0, before)
    middle_before_id = pick(to_last == 1, before)

    inner, inmost = (y > 0) & (y < 7), (y > 1) & (y < 6)
    zeros = jnp.zeros((HEADS, 2, 2, HD, HD), jnp.bfloat16)
    for ref, d, missing in ((ybuf, 0, y < 1), (ybuf, 1, y > 6), (y2buf, 0, y < 2), (y2buf, 1, y > 5)):
        @pl.when(missing)
        def _():
            ref[:, :, d] = zeros

    sends_first = jnp.logical_not((x == 3) & (core == 1))
    sends_last = jnp.logical_not((x == 0) & (core == 0))

    def sends_1(h, n):
        arrived(own.at[h, n], own_sem.at[h, n])

        @pl.when(y < 7)
        def _():
            send(own.at[h, n], ybuf.at[h, n, 0], y_sem.at[h, n], 0, up_id)

        @pl.when(y > 0)
        def _():
            send(own.at[h, n], ybuf.at[h, n, 1], y_sem.at[h, n], 0, down_id)

        for s in range(2):
            send(own.at[h, n, s], xbuf.at[h, n, 0, after_slot[s]], x_sem.at[h, n], 2, after[s])
            send(own.at[h, n, s], xbuf.at[h, n, 1, before_slot[s]], x_sem.at[h, n], 2, before[s])
        send(own.at[h, n], mate.at[h, n, pl.ds(0, 2)], mate_sem.at[h], 3, mate_id)

    def sends_2y(h, n):
        @pl.when(inner)
        def _():
            arrived(ybuf.at[h, n], y_sem.at[h, n])
            send(ybuf.at[h, n, 0], y2buf.at[h, n, 0], y2_sem.at[h], 1, up_id)
            send(ybuf.at[h, n, 1], y2buf.at[h, n, 1], y2_sem.at[h], 1, down_id)

        @pl.when(jnp.logical_not(inner))
        def _():
            arrived(ybuf.at[h, n, 0], y_sem.at[h, n])

        end = ybuf.at[h, n, 1 - core, core]
        send(end, mate.at[h, n, 2], mate_sem.at[h], 3, mate_id)

        @pl.when(relays)
        def _():
            send(end, x2buf.at[h, n, 1 - core], x2_sem.at[h, n], 9, (at(y, z, 1 - core), 3 - 3 * core))

    def sends_2x(h, n):
        arrived(xbuf.at[h, n], x_sem.at[h, n])

        @pl.when(sends_first)
        def _():
            send(xbuf.at[h, n, 0, to_first], x2buf.at[h, n, 0], x2_sem.at[h, n], 5, first_id)

        @pl.when(sends_last)
        def _():
            send(xbuf.at[h, n, 1, to_last], x2buf.at[h, n, 1], x2_sem.at[h, n], 6, last_id)

        if n == 0:
            @pl.when(after_core == 0)
            def _():
                send(xbuf.at[h, n, 0, 1 - to_first], x2buf.at[h, n, 2], middle_sem.at[h], 7, middle_after_id)
        else:
            @pl.when(before_core == 1)
            def _():
                send(xbuf.at[h, n, 1, 1 - to_last], x2buf.at[h, n, 2], middle_sem.at[h], 8, middle_before_id)

    def sends_3(h, n):
        arrived(x2buf.at[h, n, pl.ds(0, 2)], x2_sem.at[h, n])
        send(x2buf.at[h, n, 1 - core], x2buf.at[h, n, 3], pair_sem.at[h], 4, mate_id)

        @pl.when(core == n)
        def _():
            arrived(x2buf.at[h, n, 2], middle_sem.at[h])
            send(x2buf.at[h, n, 2], x2buf.at[h, n, 2], pair_sem.at[h], 4, mate_id)

    def fill_bias():
        for copy in tables:
            copy.wait()
        key_block = lax.div(lax.broadcasted_iota(jnp.int32, (HD, HD), 0), 16)
        query_block = lax.div(lax.broadcasted_iota(jnp.int32, (HD, HD), 1), 16)
        distance = key_block - query_block
        for b in range(NBANDS):
            active = jnp.zeros((HD, HD), jnp.int32)
            for block in range(BLOCKS):
                active = jnp.where(query_block == block, mask_ref[b, block], active)
            allowed = (active == 1) & (jnp.abs(distance - offset_ref[b]) < width_ref[b])
            if b == 0:
                allowed = allowed | (distance == 0)
            bias[b] = jnp.where(allowed, 0.0, NEG)
        bias[NBANDS] = jnp.full((HD, HD), NEG, jnp.float32)

    def band(b, s, step):
        source = 16 * y + x + 4 * core + 8 * s + step
        return jnp.where((source >= 0) & (source < 128), b, NBANDS)

    def attend(work, first=False):
        scores = []
        for h, s, sets in work:
            keys = jnp.concatenate([keys[...] for keys, _, _ in sets], axis=0)
            score = lax.dot_general(
                keys, query[h, s], (((1,), (1,)), ((), ())), preferred_element_type=jnp.float32
            )
            scores.append([
                score[n * HD : (n + 1) * HD] * SCALE + bias[index] for n, (_, _, index) in enumerate(sets)
            ])
        values = [[values[...] for _, values, _ in sets] for _, _, sets in work]
        peaks = [functools.reduce(jnp.maximum, score).max(axis=0, keepdims=True) for score in scores]
        if not first:
            old = [(top[h, s], total[h, s], acc[h, s]) for h, s, _ in work]
            peaks = [jnp.maximum(peak, before[0]) for peak, before in zip(peaks, old)]
        results = []
        for n, (score, peak) in enumerate(zip(scores, peaks)):
            weights = [jnp.exp2(part - peak) for part in score]
            added = functools.reduce(jnp.add, weights).sum(axis=0, keepdims=True)
            summed = [
                lax.dot_general(
                    value, weight.astype(jnp.bfloat16), (((0,), (0,)), ((), ())),
                    preferred_element_type=jnp.float32,
                )
                for value, weight in zip(values[n], weights)
            ]
            summed = functools.reduce(jnp.add, summed)
            if not first:
                kept = jnp.exp2(old[n][0] - peak)
                added, summed = old[n][1] * kept + added, old[n][2] * kept + summed
            results.append((peak, added, summed))
        for (h, s, _), (peak, added, summed) in zip(work, results):
            top[h, s], total[h, s], acc[h, s] = peak, added, summed

    def entry(ref, where, index):
        return ref.at[where(0)], ref.at[where(1)], index

    def sets_own(h, s):
        return [entry(own, lambda n: (h, n, s), 0), entry(own, lambda n: (h, n, 1 - s), 4)]

    def sets_x(h, s):
        return [
            entry(xbuf, lambda n: (h, n, 0, s), band(1, s, -1)),
            entry(xbuf, lambda n: (h, n, 1, s), band(1, s, 1)),
        ]

    def sets_y(h, s):
        return [
            entry(ybuf, lambda n: (h, n, 0, s), band(5, s, -16)),
            entry(ybuf, lambda n: (h, n, 1, s), band(5, s, 16)),
            entry(ybuf, lambda n: (h, n, s, 1 - s), band(4, s, 8 if s else -8)),
        ]

    def sets_mate(h, s):
        at_end = core == s
        other = jnp.where(at_end, 2, 1 - s)
        ends = band(3, s, 4 if s else -4)
        return [
            entry(mate, lambda n: (h, n, s), 3),
            entry(mate, lambda n: (h, n, other), jnp.where(at_end, ends, 3)),
        ]

    def sets_x2(h, s):
        earlier, later = (0, 3 - core) if s == 0 else (2 + core, 1)
        return [
            entry(x2buf, lambda n: (h, n, earlier), band(2, s, -2)),
            entry(x2buf, lambda n: (h, n, later), band(2, s, 2)),
        ]

    def sets_y2(h, s):
        return [
            entry(y2buf, lambda n: (h, n, 0, s), band(6, s, -32)),
            entry(y2buf, lambda n: (h, n, 1, s), band(6, s, 32)),
        ]

    def both(h, *kinds, first=False):
        attend([(h, s, sum((sets(h, s) for sets in kinds), [])) for s in range(2)], first)

    def wait_query(h):
        arrived(query.at[h], query_sem.at[h])

    def wait_mate(h):
        arrived(mate.at[h], mate_sem.at[h])

    def wait_x2(h):
        arrived(x2buf.at[h, 0, pl.ds(0, 3)], pair_sem.at[h])

    def wait_y2(h):
        @pl.when(inmost)
        def _():
            arrived(y2buf.at[h], y2_sem.at[h])

        @pl.when(jnp.logical_not(inmost))
        def _():
            arrived(y2buf.at[h, :, 0], y2_sem.at[h])

    def finish(h):
        columns = pl.ds(pl.multiple_of(z * COLS + h * HD, HD), HD)
        for s in range(2):
            stage[h, s] = (acc[h, s] / total[h, s]).T.astype(jnp.bfloat16)
        for dt, s in itertools.product((2, 1, 3, 0), range(2)):
            t = lax.rem(x + dt, 4)
            src = stage.at[h, s, pl.ds(pl.multiple_of(t * 32, 32), 32)]
            dst = out_ref.at[:, columns]

            def remote(sem):
                pltpu.make_async_remote_copy(
                    src_ref=src, dst_ref=dst, send_sem=sem, recv_sem=out_sem.at[0],
                    device_id=(frames[s], t), device_id_type=MESH,
                ).start()

            if dt:
                remote(out_send.at[2])
            else:
                @pl.when(frames[s] == ctx)
                def _():
                    pltpu.make_async_copy(src, dst, out_sem.at[0]).start()

                @pl.when(frames[s] != ctx)
                def _():
                    remote(out_send.at[s])

    K, V, Q = 0, 1, 2
    for h, n in ((0, K), (0, V), (1, K), (1, V), (2, K), (2, V), (0, Q), (1, Q), (2, Q)):
        spread(h, n)
    fill_bias()
    sends_1(0, K)
    sends_1(0, V)
    sends_1(1, K)
    sends_2y(0, K)
    sends_2x(0, K)
    sends_1(1, V)
    sends_2y(0, V)
    sends_2x(0, V)
    sends_1(2, K)
    sends_2y(1, K)
    sends_2x(1, K)
    sends_1(2, V)
    sends_2y(1, V)
    sends_2x(1, V)
    sends_3(0, K)
    sends_3(0, V)
    wait_query(0)
    both(0, sets_own, sets_x, sets_y, first=True)
    sends_2y(2, K)
    sends_2x(2, K)
    sends_3(1, K)
    wait_mate(0)
    wait_x2(0)
    both(0, sets_mate, sets_x2)
    wait_query(1)
    both(1, sets_own, sets_x, sets_y, first=True)
    sends_2y(2, V)
    sends_2x(2, V)
    sends_3(1, V)
    wait_y2(0)
    both(0, sets_y2)
    finish(0)
    wait_query(2)
    both(2, sets_own, sets_x, sets_y, first=True)
    wait_mate(1)
    wait_x2(1)
    wait_y2(1)
    both(1, sets_mate, sets_x2, sets_y2)
    finish(1)
    sends_3(2, K)
    sends_3(2, V)
    wait_mate(2)
    wait_y2(2)
    both(2, sets_mate, sets_y2)
    wait_x2(2)
    both(2, sets_x2)
    finish(2)

    for n, ref in ((0, k_ref), (1, v_ref), (2, q_ref)):
        part = ref.at[:, pl.ds(0, 7 * COLS)]
        arrived(part, a2a_send.at[n])

    @pl.when(jnp.logical_not(at_home))
    def _():
        part = q_ref.at[:, pl.ds(0, 3 * COLS)]
        arrived(part, a2a_send.at[3])

    for category, ref in ((2, xbuf), (3, mate), (4, x2buf.at[:, 0, pl.ds(0, 3)])):
        arrived(ref, flow_send.at[category])
    for category, ref, sent in (
        (0, ybuf, inner),
        (0, ybuf.at[:, :, 0], jnp.logical_not(inner)),
        (1, y2buf, inner),
        (5, x2buf.at[:, :, 0], sends_first),
        (6, x2buf.at[:, :, 0], sends_last),
        (7, x2buf.at[:, 0, 0], after_core == 0),
        (8, x2buf.at[:, 0, 0], before_core == 1),
        (9, x2buf.at[:, :, 0], relays),
    ):
        @pl.when(sent)
        def _():
            arrived(ref, flow_send.at[category])

    part = stage.at[:, :, pl.ds(0, 96)]
    arrived(part, out_send.at[2])
    for s in range(2):
        @pl.when(frames[s] != ctx)
        def _():
            part = stage.at[:, s, pl.ds(0, 32)]
            arrived(part, out_send.at[s])
    arrived(out_ref, out_sem.at[0])


def on_device(queries, keys, values, band_offsets, band_widths, block_mask):
    bf16 = jnp.bfloat16
    dma = pltpu.SemaphoreType.DMA
    hbm = pl.BlockSpec(memory_space=pl.ANY)
    return pl.pallas_call(
        kernel,
        out_shape=jax.ShapeDtypeStruct(queries.shape, bf16),
        in_specs=[hbm] * 6,
        out_specs=hbm,
        scratch_shapes=[
            pltpu.SMEM(band_offsets.shape, jnp.int32),
            pltpu.SMEM(band_widths.shape, jnp.int32),
            pltpu.SMEM(block_mask.shape, jnp.int32),
            pltpu.VMEM((HEADS, 2, 2, HD, HD), bf16),
            pltpu.VMEM((HEADS, 2, HD, HD), bf16),
            pltpu.VMEM((HEADS, 2, 2, 2, HD, HD), bf16),
            pltpu.VMEM((HEADS, 2, 4, HD, HD), bf16),
            pltpu.VMEM((HEADS, 2, 2, 2, HD, HD), bf16),
            pltpu.VMEM((HEADS, 2, 2, 2, HD, HD), bf16),
            pltpu.VMEM((HEADS, 2, 3, HD, HD), bf16),
            pltpu.VMEM((NBANDS + 1, HD, HD), jnp.float32),
            pltpu.VMEM((HEADS, 2, 1, HD), jnp.float32),
            pltpu.VMEM((HEADS, 2, 1, HD), jnp.float32),
            pltpu.VMEM((HEADS, 2, HD, HD), jnp.float32),
            pltpu.VMEM((HEADS, 2, HD, HD), bf16),
            dma((3,)),
            dma((HEADS, 2)),
            dma((HEADS,)),
            dma((HEADS, 2)),
            dma((HEADS, 2)),
            dma((HEADS,)),
            dma((HEADS,)),
            dma((HEADS, 2)),
            dma((HEADS,)),
            dma((HEADS,)),
            dma((1,)),
            dma((4,)),
            dma((10,)),
            dma((3,)),
        ],
        compiler_params=pltpu.CompilerParams(
            collective_id=0, has_side_effects=True, vmem_limit_bytes=60 * 2**20
        ),
    )(queries, keys, values, band_offsets, band_widths, block_mask)


def solution(mesh):
    tokens = P(("ctx", "head"), None)
    return jax.shard_map(
        on_device,
        mesh=mesh,
        in_specs=(tokens, tokens, tokens, P(), P(), P()),
        out_specs=tokens,
        check_vma=False,
    )
```

```python
import functools
import math

import jax
import jax.numpy as jnp
from jax import lax
from jax.experimental import pallas as pl
from jax.experimental.pallas import tpu as pltpu
from jax.sharding import PartitionSpec as P

HD = 128
BLOCKS = 8
NBANDS = 7
HEADS = 3
COLS = HEADS * HD
SCALE = HD ** (-0.5) * math.log2(math.e)
NEG = -1e30
MESH = pl.DeviceIdType.MESH


def place(f):
    f = lax.rem(f + 128, 128)
    return lax.rem(f, 4), lax.div(f, 16), lax.rem(lax.div(f, 4), 2), lax.rem(lax.div(f, 8), 2)


def kernel(
    q_ref, k_ref, v_ref, offset_hbm, width_hbm, mask_hbm, out_ref,
    offset_ref, width_ref, mask_ref, own, query, xbuf, x2buf, ybuf, y2buf, mate, bias, top, total, acc, stage,
    table_sem, own_sem, query_sem, x_sem, x2_sem, pair_sem, y_sem, y2_sem, mate_sem, out_sem,
    a2a_send, flow_send, out_send,
):
    ctx, x = lax.axis_index("ctx"), lax.axis_index("head")
    y, z, core = lax.div(ctx, 16), lax.rem(lax.div(ctx, 2), 8), lax.rem(ctx, 2)

    def at(y_, z_, core_):
        return (y_ * 8 + z_) * 2 + core_

    own_class = lax.rem(x + 8 - z, 4)
    frames = [16 * y + own_class + 4 * core + 8 * s for s in range(2)]
    home_class, _, home_core, home_slot = place(ctx)
    at_home = (home_class == own_class) & (home_core == core)

    def chip(class_, z_):
        return lax.rem(class_ + z_, 4)

    mate_id = (at(y, z, 1 - core), x)
    up_id = (at(lax.rem(y + 1, 8), z, core), x)
    down_id = (at(lax.rem(y + 7, 8), z, core), x)

    def neighbours(step):
        ids, slots = [], []
        for s in range(2):
            nclass, ny, ncore, nslot = place(frames[s] + step)
            ids.append((at(ny, z, ncore), chip(nclass, z)))
            slots.append(nslot)
        return ids, slots, ncore

    after, after_slot, after_core = neighbours(1)
    before, before_slot, before_core = neighbours(-1)

    barrier = pltpu.get_barrier_semaphore()

    def greet(device):
        pl.semaphore_signal(barrier, inc=1, device_id=device, device_id_type=MESH)

    def home_of(dz):
        g = lax.rem(z + dz, 8)
        return (at(y, g, home_core), chip(home_class, g))

    for dz in (4, 3, 5, 2, 6, 1, 7):
        greet(home_of(dz))
    for dt in range(1, 4):
        for s in range(2):
            greet((frames[s], lax.rem(x + dt, 4)))

    @pl.when(jnp.logical_not(at_home))
    def _():
        greet(home_of(0))

    for s in range(2):
        @pl.when(frames[s] != ctx)
        def _():
            greet((frames[s], x))

    relays = own_class == 1 + core
    takes = own_class == 3 * core

    for device in [mate_id, up_id, down_id] + after + before:
        greet(device)

    @pl.when(core == 0)
    def _():
        class_, y_, core_, _ = place(frames[0] + 3)
        greet((at(y_, z, core_), chip(class_, z)))

    @pl.when(takes)
    def _():
        greet((at(y, z, 1 - core), chip(2 - core, z)))

    tables = [
        pltpu.make_async_copy(src, dst, table_sem.at[n])
        for n, (src, dst) in enumerate(
            [(offset_hbm, offset_ref), (width_hbm, width_ref), (mask_hbm, mask_ref)]
        )
    ]
    for copy in tables:
        copy.start()
    pl.semaphore_wait(barrier, 23 - 2 * at_home.astype(jnp.int32) + relays.astype(jnp.int32) + after_core)

    token_rows = pl.ds(pl.multiple_of(x * 32, 32), 32)

    def spread(h, n):
        ref = (k_ref, v_ref, q_ref)[n]
        if n == 2:
            dst, recv = query.at[h, home_slot, token_rows], query_sem.at[h]
        else:
            dst, recv = own.at[h, n, home_slot, token_rows], own_sem.at[h, n]

        def remote(src, dz, sem):
            pltpu.make_async_remote_copy(
                src_ref=src, dst_ref=dst, send_sem=a2a_send.at[sem], recv_sem=recv,
                device_id=home_of(dz), device_id_type=MESH,
            ).start()

        for dz in (4, 3, 5, 2, 6, 1, 7, 0):
            g = lax.rem(z + dz, 8)
            src = ref.at[:, pl.ds(pl.multiple_of(g * COLS + h * HD, HD), HD)]
            if dz:
                remote(src, dz, n)
            else:
                @pl.when(at_home)
                def _():
                    pltpu.make_async_copy(src, dst, recv).start()

                @pl.when(jnp.logical_not(at_home))
                def _():
                    remote(src, dz, 3)

    def arrived(ref, sem):
        pltpu.make_async_copy(ref, ref, sem).wait()

    def send(src, dst, recv, category, device):
        pltpu.make_async_remote_copy(
            src_ref=src, dst_ref=dst, send_sem=flow_send.at[category], recv_sem=recv,
            device_id=device, device_id_type=MESH,
        ).start()

    def pick(first, pair):
        return tuple(jnp.where(first, p, q) for p, q in zip(*pair))

    to_first = jnp.where(after_slot[0] == 0, 0, 1)
    to_last = jnp.where(before_slot[1] == 1, 1, 0)
    first_id, second_id = pick(to_first == 0, after), pick(to_first == 1, after)
    first_mate_id = (first_id[0] - after_core, first_id[1])
    last_id = pick(to_last == 0, before)
    middle_id = pick(to_last == 1, before)

    inner, inmost = (y > 0) & (y < 7), (y > 1) & (y < 6)
    for ref, d, missing in ((ybuf, 0, y < 1), (ybuf, 1, y > 6), (y2buf, 0, y < 2), (y2buf, 1, y > 5)):
        @pl.when(missing)
        def _():
            part = ref.at[:, :, d] if ref is ybuf else ref.at[:, :, :, d]
            part[...] = jnp.zeros(part.shape, jnp.bfloat16)

    sends_first = jnp.logical_not((own_class == 3) & (core == 1))
    sends_last = jnp.logical_not((own_class == 0) & (core == 0))
    relay_id = (at(y, z, 1 - core), chip(3 - 3 * core, z))

    def sends_1a(h, n):
        arrived(own.at[h, n], own_sem.at[h, n])
        send(own.at[h, n, to_first], xbuf.at[h, n, 0, 0], x_sem.at[h, n, 0], 2, first_id)
        send(own.at[h, n, 1 - to_last], xbuf.at[h, n, 0, 1], x_sem.at[h, n, 0], 2, middle_id)

        @pl.when(y < 7)
        def _():
            send(own.at[h, n], ybuf.at[h, n, 0], y_sem.at[h, n], 0, up_id)

        @pl.when(y > 0)
        def _():
            send(own.at[h, n], ybuf.at[h, n, 1], y_sem.at[h, n], 0, down_id)

        send(own.at[h, n], mate.at[h, n, pl.ds(0, 2)], mate_sem.at[h], 3, mate_id)

    def sends_1b(h, n):
        send(own.at[h, n, 1 - to_first], xbuf.at[h, n, 1, 0], x_sem.at[h, n, 1], 2, second_id)
        send(own.at[h, n, to_last], xbuf.at[h, n, 1, 1], x_sem.at[h, n, 1], 2, last_id)

    def send_y2(h, n, s):
        @pl.when(inner)
        def _():
            send(ybuf.at[h, n, 0, s], y2buf.at[h, s, n, 0], y2_sem.at[h, s], 1, up_id)
            send(ybuf.at[h, n, 1, s], y2buf.at[h, s, n, 1], y2_sem.at[h, s], 1, down_id)

    def sends_2a(h, n):
        @pl.when(inner)
        def _():
            arrived(ybuf.at[h, n], y_sem.at[h, n])

        @pl.when(jnp.logical_not(inner))
        def _():
            arrived(ybuf.at[h, n, 0], y_sem.at[h, n])

        end = ybuf.at[h, n, 1 - core, core]

        @pl.when(relays)
        def _():
            send(end, x2buf.at[h, n, 1 - core], x2_sem.at[h, n, 1 - core], 8, relay_id)

        send_y2(h, n, 0)
        send(end, mate.at[h, n, 2], mate_sem.at[h], 3, mate_id)
        arrived(xbuf.at[h, n, 0], x_sem.at[h, n, 0])

        @pl.when(sends_first & (after_core == 0))
        def _():
            send(xbuf.at[h, n, 0, 0], x2buf.at[h, n, 0], x2_sem.at[h, n, 0], 5, first_id)

        @pl.when(after_core == 1)
        def _():
            send(xbuf.at[h, n, 0, 0], x2buf.at[h, n, 3], pair_sem.at[h, 0], 5, first_mate_id)

        @pl.when((before_core == 1) & (to_last == 1))
        def _():
            send(xbuf.at[h, n, 0, 1], x2buf.at[h, n, 2], pair_sem.at[h, 0], 7, middle_id)

    def sends_2b(h, n):
        arrived(xbuf.at[h, n, 1], x_sem.at[h, n, 1])

        @pl.when(sends_last)
        def _():
            send(xbuf.at[h, n, 1, 1], x2buf.at[h, n, 1], x2_sem.at[h, n, 1], 6, last_id)

        @pl.when((before_core == 1) & (to_last == 0))
        def _():
            send(xbuf.at[h, n, 1, 1], x2buf.at[h, n, 2], pair_sem.at[h, 0], 7, middle_id)

    def sends_3b(h, n):
        arrived(x2buf.at[h, n, 1], x2_sem.at[h, n, 1])

        @pl.when(core == 0)
        def _():
            send(x2buf.at[h, n, 1], x2buf.at[h, n, 3], pair_sem.at[h, 1], 4, mate_id)

    def wait_x2a(h):
        arrived(x2buf.at[h, :, 2], pair_sem.at[h, 0])

        @pl.when(core == 0)
        def _():
            for n in range(2):
                send(x2buf.at[h, n, 3], x2buf.at[h, n, 0], x2_sem.at[h, n, 0], 4, mate_id)

        @pl.when(core == 1)
        def _():
            for n in range(2):
                send(x2buf.at[h, n, 2], x2buf.at[h, n, 2], pair_sem.at[h, 1], 4, mate_id)

        for n in range(2):
            arrived(x2buf.at[h, n, 0], x2_sem.at[h, n, 0])

    def wait_x2b(h):
        arrived(x2buf.at[h, :, 2], pair_sem.at[h, 1])

    def fill_bias():
        for copy in tables:
            copy.wait()
        key_block = lax.div(lax.broadcasted_iota(jnp.int32, (HD, HD), 0), 16)
        query_block = lax.div(lax.broadcasted_iota(jnp.int32, (HD, HD), 1), 16)
        distance = key_block - query_block
        for b in range(NBANDS):
            active = jnp.zeros((HD, HD), jnp.int32)
            for block in range(BLOCKS):
                active = jnp.where(query_block == block, mask_ref[b, block], active)
            allowed = (active == 1) & (jnp.abs(distance - offset_ref[b]) < width_ref[b])
            if b == 0:
                allowed = allowed | (distance == 0)
            bias[b] = jnp.where(allowed, 0.0, NEG)
        bias[NBANDS] = jnp.full((HD, HD), NEG, jnp.float32)

    def band(b, s, step):
        source = frames[s] + step
        return jnp.where((source >= 0) & (source < 128), b, NBANDS)

    def attend(*work):
        scores = []
        for h, s, sets, _ in work:
            keys = jnp.concatenate([keys[...] for keys, _, _ in sets], axis=0)
            score = lax.dot_general(
                keys, query[h, s], (((1,), (1,)), ((), ())), preferred_element_type=jnp.float32
            )
            scores.append([
                score[n * HD : (n + 1) * HD] * SCALE + bias[index] for n, (_, _, index) in enumerate(sets)
            ])
        values = [[values[...] for _, values, _ in sets] for _, _, sets, _ in work]
        old = [None if first else (top[h, s], total[h, s], acc[h, s]) for h, s, _, first in work]
        results = []
        for score, value, before in zip(scores, values, old):
            peak = functools.reduce(jnp.maximum, score).max(axis=0, keepdims=True)
            if before:
                peak = jnp.maximum(peak, before[0])
            weights = [jnp.exp2(part - peak) for part in score]
            added = functools.reduce(jnp.add, weights).sum(axis=0, keepdims=True)
            summed = [
                lax.dot_general(
                    part, weight.astype(jnp.bfloat16), (((0,), (0,)), ((), ())),
                    preferred_element_type=jnp.float32,
                )
                for part, weight in zip(value, weights)
            ]
            summed = functools.reduce(jnp.add, summed)
            if before:
                kept = jnp.exp2(before[0] - peak)
                added, summed = before[1] * kept + added, before[2] * kept + summed
            results.append((peak, added, summed))
        for (h, s, _, _), (peak, added, summed) in zip(work, results):
            top[h, s], total[h, s], acc[h, s] = peak, added, summed

    def entry(ref, where, index):
        return ref.at[where(0)], ref.at[where(1)], index

    def sets_own(h, s):
        return [entry(own, lambda n: (h, n, s), 0), entry(own, lambda n: (h, n, 1 - s), 4)]

    def sets_x(h, s):
        return [
            entry(xbuf, lambda n: (h, n, s, 0), band(1, s, -1)),
            entry(xbuf, lambda n: (h, n, s, 1), band(1, s, 1)),
        ]

    def sets_y(h, s):
        return [
            entry(ybuf, lambda n: (h, n, 0, s), band(5, s, -16)),
            entry(ybuf, lambda n: (h, n, 1, s), band(5, s, 16)),
            entry(ybuf, lambda n: (h, n, s, 1 - s), band(4, s, 8 if s else -8)),
        ]

    def sets_mate(h, s):
        at_end = core == s
        other = jnp.where(at_end, 2, 1 - s)
        ends = band(3, s, 4 if s else -4)
        return [
            entry(mate, lambda n: (h, n, s), 3),
            entry(mate, lambda n: (h, n, other), jnp.where(at_end, ends, 3)),
        ]

    def sets_x2(h, s):
        earlier, later = (0, 3 - core) if s == 0 else (2 + core, 1)
        return [
            entry(x2buf, lambda n: (h, n, earlier), band(2, s, -2)),
            entry(x2buf, lambda n: (h, n, later), band(2, s, 2)),
        ]

    def sets_y2(h, s):
        return [
            entry(y2buf, lambda n: (h, s, n, 0), band(6, s, -32)),
            entry(y2buf, lambda n: (h, s, n, 1), band(6, s, 32)),
        ]

    def near(s, h, *more):
        return h, s, sum((sets(h, s) for sets in (sets_own, sets_x, sets_y) + more), []), True

    def far(s, h, *more):
        return h, s, sum((sets(h, s) for sets in more + (sets_x2, sets_y2)), []), False

    def wait_query(h):
        arrived(query.at[h], query_sem.at[h])

    def wait_mate(h):
        arrived(mate.at[h], mate_sem.at[h])

    def wait_y2(h, s):
        @pl.when(inmost)
        def _():
            arrived(y2buf.at[h, s], y2_sem.at[h, s])

        @pl.when(jnp.logical_not(inmost))
        def _():
            arrived(y2buf.at[h, s, :, 0], y2_sem.at[h, s])

    def finish(s, h):
        columns = pl.ds(pl.multiple_of(z * COLS + h * HD, HD), HD)
        stage[h, s] = (acc[h, s] / total[h, s]).T.astype(jnp.bfloat16)
        for dt in (2, 1, 3, 0):
            t = lax.rem(x + dt, 4)
            src = stage.at[h, s, pl.ds(pl.multiple_of(t * 32, 32), 32)]
            dst = out_ref.at[:, columns]

            def remote(sem):
                pltpu.make_async_remote_copy(
                    src_ref=src, dst_ref=dst, send_sem=sem, recv_sem=out_sem.at[0],
                    device_id=(frames[s], t), device_id_type=MESH,
                ).start()

            if dt:
                remote(out_send.at[2])
            else:
                @pl.when(frames[s] == ctx)
                def _():
                    pltpu.make_async_copy(src, dst, out_sem.at[0]).start()

                @pl.when(frames[s] != ctx)
                def _():
                    remote(out_send.at[s])

    K, V, Q = 0, 1, 2
    for h, n in ((0, K), (0, V), (1, K), (1, V), (2, K), (2, V), (0, Q), (1, Q), (2, Q)):
        spread(h, n)
    fill_bias()
    sends_1a(0, K)
    sends_1a(0, V)
    sends_1a(1, K)
    sends_2a(0, K)
    sends_1b(0, K)
    sends_1a(1, V)
    sends_2a(0, V)
    sends_1b(0, V)
    sends_1a(2, K)
    sends_2a(1, K)
    sends_1a(2, V)
    sends_2a(1, V)
    sends_1b(1, K)
    sends_1b(1, V)
    sends_2b(0, K)
    sends_2b(0, V)
    send_y2(0, K, 1)
    send_y2(0, V, 1)
    wait_query(0)
    wait_query(1)
    wait_mate(0)
    attend(near(0, 0), near(0, 1), near(1, 0, sets_mate))
    sends_2a(2, K)
    sends_1b(2, K)
    sends_2a(2, V)
    sends_1b(2, V)
    for h in (1, 2):
        send_y2(h, K, 1)
        send_y2(h, V, 1)
    sends_2b(1, K)
    sends_2b(1, V)
    sends_3b(0, K)
    sends_3b(0, V)
    wait_query(2)
    wait_mate(1)
    wait_y2(0, 0)
    wait_x2a(0)
    attend(far(0, 0, sets_mate), near(0, 2), near(1, 1, sets_mate))
    finish(0, 0)
    wait_y2(1, 0)
    wait_x2a(1)
    attend(far(0, 1, sets_mate))
    finish(0, 1)
    sends_2b(2, K)
    sends_2b(2, V)
    wait_mate(2)
    wait_y2(2, 0)
    wait_x2a(2)
    attend(far(0, 2, sets_mate))
    finish(0, 2)
    sends_3b(1, K)
    sends_3b(1, V)
    wait_y2(0, 1)
    wait_x2b(0)
    wait_y2(1, 1)
    wait_x2b(1)
    attend(far(1, 0), far(1, 1), near(1, 2, sets_mate))
    finish(1, 0)
    finish(1, 1)
    sends_3b(2, K)
    sends_3b(2, V)
    wait_y2(2, 1)
    wait_x2b(2)
    attend(far(1, 2))
    finish(1, 2)

    for n, ref in ((0, k_ref), (1, v_ref), (2, q_ref)):
        part = ref.at[:, pl.ds(0, 7 * COLS)]
        arrived(part, a2a_send.at[n])

    @pl.when(jnp.logical_not(at_home))
    def _():
        part = q_ref.at[:, pl.ds(0, 3 * COLS)]
        arrived(part, a2a_send.at[3])

    arrived(xbuf, flow_send.at[2])
    arrived(mate, flow_send.at[3])
    for category, ref, sent in (
        (0, ybuf, inner),
        (0, ybuf.at[:, :, 0], jnp.logical_not(inner)),
        (1, y2buf, inner),
        (4, x2buf.at[:, :, pl.ds(0, 2)], core == 0),
        (4, x2buf.at[:, :, 0], core == 1),
        (5, x2buf.at[:, :, 0], sends_first),
        (6, x2buf.at[:, :, 0], sends_last),
        (7, x2buf.at[:, :, 0], before_core == 1),
        (8, x2buf.at[:, :, 0], relays),
    ):
        @pl.when(sent)
        def _():
            arrived(ref, flow_send.at[category])

    part = stage.at[:, :, pl.ds(0, 96)]
    arrived(part, out_send.at[2])
    for s in range(2):
        @pl.when(frames[s] != ctx)
        def _():
            part = stage.at[:, s, pl.ds(0, 32)]
            arrived(part, out_send.at[s])
    arrived(out_ref, out_sem.at[0])


def on_device(queries, keys, values, band_offsets, band_widths, block_mask):
    bf16 = jnp.bfloat16
    dma = pltpu.SemaphoreType.DMA
    hbm = pl.BlockSpec(memory_space=pl.ANY)
    return pl.pallas_call(
        kernel,
        out_shape=jax.ShapeDtypeStruct(queries.shape, bf16),
        in_specs=[hbm] * 6,
        out_specs=hbm,
        scratch_shapes=[
            pltpu.SMEM(band_offsets.shape, jnp.int32),
            pltpu.SMEM(band_widths.shape, jnp.int32),
            pltpu.SMEM(block_mask.shape, jnp.int32),
            pltpu.VMEM((HEADS, 2, 2, HD, HD), bf16),
            pltpu.VMEM((HEADS, 2, HD, HD), bf16),
            pltpu.VMEM((HEADS, 2, 2, 2, HD, HD), bf16),
            pltpu.VMEM((HEADS, 2, 4, HD, HD), bf16),
            pltpu.VMEM((HEADS, 2, 2, 2, HD, HD), bf16),
            pltpu.VMEM((HEADS, 2, 2, 2, HD, HD), bf16),
            pltpu.VMEM((HEADS, 2, 3, HD, HD), bf16),
            pltpu.VMEM((NBANDS + 1, HD, HD), jnp.float32),
            pltpu.VMEM((HEADS, 2, 1, HD), jnp.float32),
            pltpu.VMEM((HEADS, 2, 1, HD), jnp.float32),
            pltpu.VMEM((HEADS, 2, HD, HD), jnp.float32),
            pltpu.VMEM((HEADS, 2, HD, HD), bf16),
            dma((3,)),
            dma((HEADS, 2)),
            dma((HEADS,)),
            dma((HEADS, 2, 2)),
            dma((HEADS, 2, 2)),
            dma((HEADS, 2)),
            dma((HEADS, 2)),
            dma((HEADS, 2)),
            dma((HEADS,)),
            dma((1,)),
            dma((4,)),
            dma((9,)),
            dma((3,)),
        ],
        compiler_params=pltpu.CompilerParams(
            collective_id=0, has_side_effects=True, vmem_limit_bytes=60 * 2**20
        ),
    )(queries, keys, values, band_offsets, band_widths, block_mask)


def solution(mesh):
    tokens = P(("ctx", "head"), None)
    return jax.shard_map(
        on_device,
        mesh=mesh,
        in_specs=(tokens, tokens, tokens, P(), P(), P()),
        out_specs=tokens,
        check_vma=False,
    )
```

```python
import functools
import math

import jax
import jax.numpy as jnp
from jax import lax
from jax.experimental import pallas as pl
from jax.experimental.pallas import tpu as pltpu
from jax.sharding import PartitionSpec as P

HD = 128
BLOCKS = 8
NBANDS = 7
HEADS = 3
COLS = HEADS * HD
SCALE = HD ** (-0.5) * math.log2(math.e)
NEG = -1e30
MESH = pl.DeviceIdType.MESH


def place(f):
    f = lax.rem(f + 128, 128)
    return lax.rem(f, 4), lax.div(f, 16), lax.rem(lax.div(f, 4), 2), lax.rem(lax.div(f, 8), 2)


def kernel(
    q_ref, k_ref, v_ref, offset_hbm, width_hbm, mask_hbm, out_ref,
    offset_ref, width_ref, mask_ref, own, query, xbuf, x2buf, ybuf, y2buf, mate, bias, top, total, acc, stage,
    table_sem, own_sem, query_sem, x_sem, x2_sem, pair_sem, y_sem, y2_sem, mate_sem, out_sem,
    a2a_send, flow_send, out_send,
):
    ctx, x = lax.axis_index("ctx"), lax.axis_index("head")
    y, z, core = lax.div(ctx, 16), lax.rem(lax.div(ctx, 2), 8), lax.rem(ctx, 2)

    def at(y_, z_, core_):
        return (y_ * 8 + z_) * 2 + core_

    own_class = lax.rem(x + z, 4)
    frames = [16 * y + own_class + 4 * core + 8 * s for s in range(2)]
    home_class, _, home_core, home_slot = place(ctx)
    at_home = (home_class == own_class) & (home_core == core)

    def chip(class_, z_):
        return lax.rem(class_ + 8 - z_, 4)

    mate_id = (at(y, z, 1 - core), x)
    up_id = (at(lax.rem(y + 1, 8), z, core), x)
    down_id = (at(lax.rem(y + 7, 8), z, core), x)

    def neighbours(step):
        ids, slots = [], []
        for s in range(2):
            nclass, ny, ncore, nslot = place(frames[s] + step)
            ids.append((at(ny, z, ncore), chip(nclass, z)))
            slots.append(nslot)
        return ids, slots, ncore

    after, after_slot, after_core = neighbours(1)
    before, before_slot, before_core = neighbours(-1)

    barrier = pltpu.get_barrier_semaphore()

    def greet(device):
        pl.semaphore_signal(barrier, inc=1, device_id=device, device_id_type=MESH)

    def home_of(dz):
        g = lax.rem(z + dz, 8)
        return (at(y, g, home_core), chip(home_class, g))

    for dz in (4, 3, 5, 2, 6, 1, 7):
        greet(home_of(dz))
    for dt in range(1, 4):
        for s in range(2):
            greet((frames[s], lax.rem(x + dt, 4)))

    @pl.when(jnp.logical_not(at_home))
    def _():
        greet(home_of(0))

    for s in range(2):
        @pl.when(frames[s] != ctx)
        def _():
            greet((frames[s], x))

    relays = own_class == 1 + core
    takes = own_class == 3 * core

    for device in [mate_id, up_id, down_id] + after + before:
        greet(device)

    @pl.when(core == 0)
    def _():
        class_, y_, core_, _ = place(frames[0] + 3)
        greet((at(y_, z, core_), chip(class_, z)))

    @pl.when(takes)
    def _():
        greet((at(y, z, 1 - core), chip(2 - core, z)))

    tables = [
        pltpu.make_async_copy(src, dst, table_sem.at[n])
        for n, (src, dst) in enumerate(
            [(offset_hbm, offset_ref), (width_hbm, width_ref), (mask_hbm, mask_ref)]
        )
    ]
    for copy in tables:
        copy.start()
    pl.semaphore_wait(barrier, 23 - 2 * at_home.astype(jnp.int32) + relays.astype(jnp.int32) + after_core)

    token_rows = pl.ds(pl.multiple_of(x * 32, 32), 32)

    def spread(h, n):
        ref = (k_ref, v_ref, q_ref)[n]
        if n == 2:
            dst, recv = query.at[h, home_slot, token_rows], query_sem.at[h]
        else:
            dst, recv = own.at[h, n, home_slot, token_rows], own_sem.at[h, n]

        def remote(src, dz, sem):
            pltpu.make_async_remote_copy(
                src_ref=src, dst_ref=dst, send_sem=a2a_send.at[sem], recv_sem=recv,
                device_id=home_of(dz), device_id_type=MESH,
            ).start()

        for dz in (4, 3, 5, 2, 6, 1, 7, 0):
            g = lax.rem(z + dz, 8)
            src = ref.at[:, pl.ds(pl.multiple_of(g * COLS + h * HD, HD), HD)]
            if dz:
                remote(src, dz, n)
            else:
                @pl.when(at_home)
                def _():
                    pltpu.make_async_copy(src, dst, recv).start()

                @pl.when(jnp.logical_not(at_home))
                def _():
                    remote(src, dz, 3)

    def arrived(ref, sem):
        pltpu.make_async_copy(ref, ref, sem).wait()

    def send(src, dst, recv, category, device):
        pltpu.make_async_remote_copy(
            src_ref=src, dst_ref=dst, send_sem=flow_send.at[category], recv_sem=recv,
            device_id=device, device_id_type=MESH,
        ).start()

    def pick(first, pair):
        return tuple(jnp.where(first, p, q) for p, q in zip(*pair))

    to_first = jnp.where(after_slot[0] == 0, 0, 1)
    to_last = jnp.where(before_slot[1] == 1, 1, 0)
    first_id, second_id = pick(to_first == 0, after), pick(to_first == 1, after)
    first_mate_id = (first_id[0] - after_core, first_id[1])
    last_id = pick(to_last == 0, before)
    middle_id = pick(to_last == 1, before)

    inner, inmost = (y > 0) & (y < 7), (y > 1) & (y < 6)
    for ref, d, missing in ((ybuf, 0, y < 1), (ybuf, 1, y > 6), (y2buf, 0, y < 2), (y2buf, 1, y > 5)):
        @pl.when(missing)
        def _():
            part = ref.at[:, :, d] if ref is ybuf else ref.at[:, :, :, d]
            part[...] = jnp.zeros(part.shape, jnp.bfloat16)

    sends_first = jnp.logical_not((own_class == 3) & (core == 1))
    sends_last = jnp.logical_not((own_class == 0) & (core == 0))
    relay_id = (at(y, z, 1 - core), chip(3 - 3 * core, z))

    def sends_1a(h, n):
        arrived(own.at[h, n], own_sem.at[h, n])
        send(own.at[h, n, to_first], xbuf.at[h, n, 0, 0], x_sem.at[h, n, 0], 2, first_id)
        send(own.at[h, n, 1 - to_last], xbuf.at[h, n, 0, 1], x_sem.at[h, n, 0], 2, middle_id)

        @pl.when(y < 7)
        def _():
            send(own.at[h, n], ybuf.at[h, n, 0], y_sem.at[h, n], 0, up_id)

        @pl.when(y > 0)
        def _():
            send(own.at[h, n], ybuf.at[h, n, 1], y_sem.at[h, n], 0, down_id)

        send(own.at[h, n], mate.at[h, n, pl.ds(0, 2)], mate_sem.at[h], 3, mate_id)

    def sends_1b(h, n):
        send(own.at[h, n, 1 - to_first], xbuf.at[h, n, 1, 0], x_sem.at[h, n, 1], 2, second_id)
        send(own.at[h, n, to_last], xbuf.at[h, n, 1, 1], x_sem.at[h, n, 1], 2, last_id)

    def send_y2(h, n, s):
        @pl.when(inner)
        def _():
            send(ybuf.at[h, n, 0, s], y2buf.at[h, s, n, 0], y2_sem.at[h, s], 1, up_id)
            send(ybuf.at[h, n, 1, s], y2buf.at[h, s, n, 1], y2_sem.at[h, s], 1, down_id)

    def sends_2a(h, n):
        @pl.when(inner)
        def _():
            arrived(ybuf.at[h, n], y_sem.at[h, n])

        @pl.when(jnp.logical_not(inner))
        def _():
            arrived(ybuf.at[h, n, 0], y_sem.at[h, n])

        end = ybuf.at[h, n, 1 - core, core]

        @pl.when(relays)
        def _():
            send(end, x2buf.at[h, n, 1 - core], x2_sem.at[h, n, 1 - core], 8, relay_id)

        send_y2(h, n, 0)
        send(end, mate.at[h, n, 2], mate_sem.at[h], 3, mate_id)
        arrived(xbuf.at[h, n, 0], x_sem.at[h, n, 0])

        @pl.when(sends_first & (after_core == 0))
        def _():
            send(xbuf.at[h, n, 0, 0], x2buf.at[h, n, 0], x2_sem.at[h, n, 0], 5, first_id)

        @pl.when(after_core == 1)
        def _():
            send(xbuf.at[h, n, 0, 0], x2buf.at[h, n, 3], pair_sem.at[h, 0], 5, first_mate_id)

        @pl.when((before_core == 1) & (to_last == 1))
        def _():
            send(xbuf.at[h, n, 0, 1], x2buf.at[h, n, 2], pair_sem.at[h, 0], 7, middle_id)

    def sends_2b(h, n):
        arrived(xbuf.at[h, n, 1], x_sem.at[h, n, 1])

        @pl.when(sends_last)
        def _():
            send(xbuf.at[h, n, 1, 1], x2buf.at[h, n, 1], x2_sem.at[h, n, 1], 6, last_id)

        @pl.when((before_core == 1) & (to_last == 0))
        def _():
            send(xbuf.at[h, n, 1, 1], x2buf.at[h, n, 2], pair_sem.at[h, 0], 7, middle_id)

    def sends_3b(h, n):
        arrived(x2buf.at[h, n, 1], x2_sem.at[h, n, 1])

        @pl.when(core == 0)
        def _():
            send(x2buf.at[h, n, 1], x2buf.at[h, n, 3], pair_sem.at[h, 1], 4, mate_id)

    def wait_x2a(h):
        arrived(x2buf.at[h, :, 2], pair_sem.at[h, 0])

        @pl.when(core == 0)
        def _():
            for n in range(2):
                send(x2buf.at[h, n, 3], x2buf.at[h, n, 0], x2_sem.at[h, n, 0], 4, mate_id)

        @pl.when(core == 1)
        def _():
            for n in range(2):
                send(x2buf.at[h, n, 2], x2buf.at[h, n, 2], pair_sem.at[h, 1], 4, mate_id)

        for n in range(2):
            arrived(x2buf.at[h, n, 0], x2_sem.at[h, n, 0])

    def wait_x2b(h):
        arrived(x2buf.at[h, :, 2], pair_sem.at[h, 1])

    def fill_bias():
        for copy in tables:
            copy.wait()
        key_block = lax.div(lax.broadcasted_iota(jnp.int32, (HD, HD), 0), 16)
        query_block = lax.div(lax.broadcasted_iota(jnp.int32, (HD, HD), 1), 16)
        distance = key_block - query_block
        for b in range(NBANDS):
            active = jnp.zeros((HD, HD), jnp.int32)
            for block in range(BLOCKS):
                active = jnp.where(query_block == block, mask_ref[b, block], active)
            allowed = (active == 1) & (jnp.abs(distance - offset_ref[b]) < width_ref[b])
            if b == 0:
                allowed = allowed | (distance == 0)
            bias[b] = jnp.where(allowed, 0.0, NEG)
        bias[NBANDS] = jnp.full((HD, HD), NEG, jnp.float32)

    def band(b, s, step):
        source = frames[s] + step
        return jnp.where((source >= 0) & (source < 128), b, NBANDS)

    def attend(*work):
        scores = []
        for h, s, sets, _ in work:
            keys = jnp.concatenate([keys[...] for keys, _, _ in sets], axis=0)
            score = lax.dot_general(
                keys, query[h, s], (((1,), (1,)), ((), ())), preferred_element_type=jnp.float32
            )
            scores.append([
                score[n * HD : (n + 1) * HD] * SCALE + bias[index] for n, (_, _, index) in enumerate(sets)
            ])
        values = [[values[...] for _, values, _ in sets] for _, _, sets, _ in work]
        old = [None if first else (top[h, s], total[h, s], acc[h, s]) for h, s, _, first in work]
        results = []
        for score, value, before in zip(scores, values, old):
            peak = functools.reduce(jnp.maximum, score).max(axis=0, keepdims=True)
            if before:
                peak = jnp.maximum(peak, before[0])
            weights = [jnp.exp2(part - peak) for part in score]
            added = functools.reduce(jnp.add, weights).sum(axis=0, keepdims=True)
            summed = [
                lax.dot_general(
                    part, weight.astype(jnp.bfloat16), (((0,), (0,)), ((), ())),
                    preferred_element_type=jnp.float32,
                )
                for part, weight in zip(value, weights)
            ]
            summed = functools.reduce(jnp.add, summed)
            if before:
                kept = jnp.exp2(before[0] - peak)
                added, summed = before[1] * kept + added, before[2] * kept + summed
            results.append((peak, added, summed))
        for (h, s, _, _), (peak, added, summed) in zip(work, results):
            top[h, s], total[h, s], acc[h, s] = peak, added, summed

    def entry(ref, where, index):
        return ref.at[where(0)], ref.at[where(1)], index

    def sets_own(h, s):
        return [entry(own, lambda n: (h, n, s), 0), entry(own, lambda n: (h, n, 1 - s), 4)]

    def sets_x(h, s):
        return [
            entry(xbuf, lambda n: (h, n, s, 0), band(1, s, -1)),
            entry(xbuf, lambda n: (h, n, s, 1), band(1, s, 1)),
        ]

    def sets_y(h, s):
        return [
            entry(ybuf, lambda n: (h, n, 0, s), band(5, s, -16)),
            entry(ybuf, lambda n: (h, n, 1, s), band(5, s, 16)),
            entry(ybuf, lambda n: (h, n, s, 1 - s), band(4, s, 8 if s else -8)),
        ]

    def sets_mate(h, s):
        at_end = core == s
        other = jnp.where(at_end, 2, 1 - s)
        ends = band(3, s, 4 if s else -4)
        return [
            entry(mate, lambda n: (h, n, s), 3),
            entry(mate, lambda n: (h, n, other), jnp.where(at_end, ends, 3)),
        ]

    def sets_x2(h, s):
        earlier, later = (0, 3 - core) if s == 0 else (2 + core, 1)
        return [
            entry(x2buf, lambda n: (h, n, earlier), band(2, s, -2)),
            entry(x2buf, lambda n: (h, n, later), band(2, s, 2)),
        ]

    def sets_y2(h, s):
        return [
            entry(y2buf, lambda n: (h, s, n, 0), band(6, s, -32)),
            entry(y2buf, lambda n: (h, s, n, 1), band(6, s, 32)),
        ]

    def near(s, h, *more):
        return h, s, sum((sets(h, s) for sets in (sets_own, sets_x, sets_y) + more), []), True

    def far(s, h, *more):
        return h, s, sum((sets(h, s) for sets in more + (sets_x2, sets_y2)), []), False

    def wait_query(h):
        arrived(query.at[h], query_sem.at[h])

    def wait_mate(h):
        arrived(mate.at[h], mate_sem.at[h])

    def wait_y2(h, s):
        @pl.when(inmost)
        def _():
            arrived(y2buf.at[h, s], y2_sem.at[h, s])

        @pl.when(jnp.logical_not(inmost))
        def _():
            arrived(y2buf.at[h, s, :, 0], y2_sem.at[h, s])

    def finish(s, h):
        columns = pl.ds(pl.multiple_of(z * COLS + h * HD, HD), HD)
        stage[h, s] = (acc[h, s] / total[h, s]).T.astype(jnp.bfloat16)
        for dt in (2, 1, 3, 0):
            t = lax.rem(x + dt, 4)
            src = stage.at[h, s, pl.ds(pl.multiple_of(t * 32, 32), 32)]
            dst = out_ref.at[:, columns]

            def remote(sem):
                pltpu.make_async_remote_copy(
                    src_ref=src, dst_ref=dst, send_sem=sem, recv_sem=out_sem.at[0],
                    device_id=(frames[s], t), device_id_type=MESH,
                ).start()

            if dt:
                remote(out_send.at[2])
            else:
                @pl.when(frames[s] == ctx)
                def _():
                    pltpu.make_async_copy(src, dst, out_sem.at[0]).start()

                @pl.when(frames[s] != ctx)
                def _():
                    remote(out_send.at[s])

    K, V, Q = 0, 1, 2
    for h, n in ((0, K), (0, V), (1, K), (1, V), (2, K), (2, V), (0, Q), (1, Q), (2, Q)):
        spread(h, n)
    fill_bias()
    sends_1a(0, K)
    sends_1a(0, V)
    sends_1a(1, K)
    sends_2a(0, K)
    sends_1b(0, K)
    sends_1a(1, V)
    sends_2a(0, V)
    sends_1b(0, V)
    sends_1a(2, K)
    sends_2a(1, K)
    sends_1a(2, V)
    sends_2a(1, V)
    sends_1b(1, K)
    sends_1b(1, V)
    sends_2b(0, K)
    sends_2b(0, V)
    send_y2(0, K, 1)
    send_y2(0, V, 1)
    wait_query(0)
    wait_query(1)
    wait_mate(0)
    attend(near(0, 0), near(0, 1), near(1, 0, sets_mate))
    sends_2a(2, K)
    sends_2a(2, V)
    sends_1b(2, K)
    sends_1b(2, V)
    for h in (1, 2):
        send_y2(h, K, 1)
        send_y2(h, V, 1)
    sends_2b(1, K)
    sends_2b(1, V)
    sends_3b(0, K)
    sends_3b(0, V)
    wait_query(2)
    wait_mate(1)
    wait_y2(0, 0)
    wait_x2a(0)
    attend(far(0, 0, sets_mate), near(0, 2), near(1, 1, sets_mate))
    finish(0, 0)
    wait_y2(1, 0)
    wait_x2a(1)
    attend(far(0, 1, sets_mate))
    finish(0, 1)
    sends_2b(2, K)
    sends_2b(2, V)
    wait_mate(2)
    wait_y2(2, 0)
    wait_x2a(2)
    attend(far(0, 2, sets_mate))
    finish(0, 2)
    sends_3b(1, K)
    sends_3b(1, V)
    wait_y2(0, 1)
    wait_x2b(0)
    wait_y2(1, 1)
    wait_x2b(1)
    attend(far(1, 0), far(1, 1), near(1, 2, sets_mate))
    finish(1, 0)
    finish(1, 1)
    sends_3b(2, K)
    sends_3b(2, V)
    wait_y2(2, 1)
    wait_x2b(2)
    attend(far(1, 2))
    finish(1, 2)

    for n, ref in ((0, k_ref), (1, v_ref), (2, q_ref)):
        part = ref.at[:, pl.ds(0, 7 * COLS)]
        arrived(part, a2a_send.at[n])

    @pl.when(jnp.logical_not(at_home))
    def _():
        part = q_ref.at[:, pl.ds(0, 3 * COLS)]
        arrived(part, a2a_send.at[3])

    arrived(xbuf, flow_send.at[2])
    arrived(mate, flow_send.at[3])
    for category, ref, sent in (
        (0, ybuf, inner),
        (0, ybuf.at[:, :, 0], jnp.logical_not(inner)),
        (1, y2buf, inner),
        (4, x2buf.at[:, :, pl.ds(0, 2)], core == 0),
        (4, x2buf.at[:, :, 0], core == 1),
        (5, x2buf.at[:, :, 0], sends_first),
        (6, x2buf.at[:, :, 0], sends_last),
        (7, x2buf.at[:, :, 0], before_core == 1),
        (8, x2buf.at[:, :, 0], relays),
    ):
        @pl.when(sent)
        def _():
            arrived(ref, flow_send.at[category])

    part = stage.at[:, :, pl.ds(0, 96)]
    arrived(part, out_send.at[2])
    for s in range(2):
        @pl.when(frames[s] != ctx)
        def _():
            part = stage.at[:, s, pl.ds(0, 32)]
            arrived(part, out_send.at[s])
    arrived(out_ref, out_sem.at[0])


def on_device(queries, keys, values, band_offsets, band_widths, block_mask):
    bf16 = jnp.bfloat16
    dma = pltpu.SemaphoreType.DMA
    hbm = pl.BlockSpec(memory_space=pl.ANY)
    return pl.pallas_call(
        kernel,
        out_shape=jax.ShapeDtypeStruct(queries.shape, bf16),
        in_specs=[hbm] * 6,
        out_specs=hbm,
        scratch_shapes=[
            pltpu.SMEM(band_offsets.shape, jnp.int32),
            pltpu.SMEM(band_widths.shape, jnp.int32),
            pltpu.SMEM(block_mask.shape, jnp.int32),
            pltpu.VMEM((HEADS, 2, 2, HD, HD), bf16),
            pltpu.VMEM((HEADS, 2, HD, HD), bf16),
            pltpu.VMEM((HEADS, 2, 2, 2, HD, HD), bf16),
            pltpu.VMEM((HEADS, 2, 4, HD, HD), bf16),
            pltpu.VMEM((HEADS, 2, 2, 2, HD, HD), bf16),
            pltpu.VMEM((HEADS, 2, 2, 2, HD, HD), bf16),
            pltpu.VMEM((HEADS, 2, 3, HD, HD), bf16),
            pltpu.VMEM((NBANDS + 1, HD, HD), jnp.float32),
            pltpu.VMEM((HEADS, 2, 1, HD), jnp.float32),
            pltpu.VMEM((HEADS, 2, 1, HD), jnp.float32),
            pltpu.VMEM((HEADS, 2, HD, HD), jnp.float32),
            pltpu.VMEM((HEADS, 2, HD, HD), bf16),
            dma((3,)),
            dma((HEADS, 2)),
            dma((HEADS,)),
            dma((HEADS, 2, 2)),
            dma((HEADS, 2, 2)),
            dma((HEADS, 2)),
            dma((HEADS, 2)),
            dma((HEADS, 2)),
            dma((HEADS,)),
            dma((1,)),
            dma((4,)),
            dma((9,)),
            dma((3,)),
        ],
        compiler_params=pltpu.CompilerParams(
            collective_id=0, has_side_effects=True, vmem_limit_bytes=60 * 2**20
        ),
    )(queries, keys, values, band_offsets, band_widths, block_mask)


def solution(mesh):
    tokens = P(("ctx", "head"), None)
    return jax.shard_map(
        on_device,
        mesh=mesh,
        in_specs=(tokens, tokens, tokens, P(), P(), P()),
        out_specs=tokens,
        check_vma=False,
    )
```
